32 devices in a mesh: dp: 16 (over z, x, core), sub: 2 (over y).
Axes of the slice: x: 2, y: 2, z: 4, core: 2. Of those that a mesh axis runs over, the one named last changes fastest.
Arguments:
- picture_encoder_embeds: float32 [4096, 1152], P(('dp', 'sub')), may hold values from -0.24 to 0.24
- caption_encoder_embeds: float32 [4096, 1152], P(('dp', 'sub')), may hold values from -0.24 to 0.24
- score_multiplier: float32 [], replicated, may hold values from 2 to 10
- score_offset_term: float32 [], replicated, may hold values from -4 to -1
Outputs:
- image_grad: float32 [4096, 1152], P(('dp', 'sub'))
- text_grad: float32 [4096, 1152], P(('dp', 'sub'))
The draws below stay inside these ranges and needn't reach their ends.
All inputs are finite; a program needn't handle non-finite values.
Results may differ from the reference program's by a relative error of at most 0.005.
Values may be sent and summed in bfloat16 or wider, within the bound.
A program may use at most 64 MiB of HBM per device.

```python
import math
import jax
import jax.numpy as jnp
from jax import lax

D = 1152
GROUP = 256
BLOCKS = 16
PAIRS = 4096


def levels(rng, shape, cuts, smallest, top_value):
    gain = 1.0
    for dim, blocks in cuts:
        steps = jax.random.uniform(jax.random.fold_in(jax.random.fold_in(rng, 6), dim), (blocks,), jnp.float32, smallest / len(cuts), top_value / len(cuts))
        gain = gain * jnp.repeat(jnp.exp(steps), shape[dim] // blocks).reshape((-1,) + (1,) * (len(shape) - 1 - dim))
    return gain


def noise(rng, shape, deviation, most, cuts=(), kind=jnp.bfloat16):
    result = deviation * jax.random.normal(rng, shape, jnp.float32)
    if cuts:
        result = result * levels(rng, shape, cuts, -0.22, 0.18)
    return jnp.clip(result, -most, most).astype(kind)


def setup_inputs(seed: int = 0) -> dict:
    arg_keys = jax.random.split(jax.random.key(seed), 5)
    return {
        "picture_encoder_embeds": noise(arg_keys[0], (PAIRS, D), 0.03, 0.24, ((0, 32),), jnp.float32),
        "caption_encoder_embeds": noise(arg_keys[1], (PAIRS, D), 0.03, 0.24, ((0, 32),), jnp.float32),
        "score_multiplier": jnp.clip(jnp.exp(jax.random.uniform(arg_keys[2], (), jnp.float32, math.log(2.0), math.log(10.0))), 2.0, 10.0),
        "score_offset_term": jnp.clip(jax.random.uniform(arg_keys[3], (), jnp.float32, -4.0, -1.0), -4.0, -1.0),
    }


def normalize(values):
    inverse = lax.rsqrt(lax.optimization_barrier(jnp.sum(values * values, axis=-1, keepdims=True)) + 1e-06)
    return (values * inverse, inverse)

def backward_norm(unit, inverse, direction):
    return (direction - unit * lax.optimization_barrier(jnp.sum(unit * direction, axis=-1, keepdims=True))) * inverse

def reference(picture_encoder_embeds, caption_encoder_embeds, score_multiplier, score_offset_term):
    image_unit, image_inverse = normalize(picture_encoder_embeds)
    text_unit, text_inverse = normalize(caption_encoder_embeds)
    picture_first_index = image_unit.astype(jnp.bfloat16)
    text_low = text_unit.astype(jnp.bfloat16)
    text_groups = text_low.reshape(BLOCKS, GROUP, D)
    window = jnp.concatenate([jnp.roll(text_groups, 1, axis=0), text_groups, jnp.roll(text_groups, -1, axis=0)], axis=1)
    image_groups = picture_first_index.reshape(BLOCKS, GROUP, D)
    row_ids = lax.broadcasted_iota(jnp.int32, (GROUP, 3 * GROUP), 0)
    col_ids = lax.broadcasted_iota(jnp.int32, (GROUP, 3 * GROUP), 1)
    match_sign_label = jnp.where(col_ids == row_ids + GROUP, jnp.float32(1.0), jnp.float32(-1.0))

    def per_block(block_args):
        earlier_entries, later_entries = block_args
        similarity_scores = score_multiplier * jnp.dot(earlier_entries, later_entries.T, preferred_element_type=jnp.float32) + score_offset_term
        derivative_weights = (-match_sign_label * score_multiplier * jax.nn.sigmoid(-match_sign_label * similarity_scores)).astype(jnp.bfloat16)
        image_part = jnp.dot(derivative_weights, later_entries, preferred_element_type=jnp.float32)
        window_part = jnp.dot(derivative_weights.T, earlier_entries, preferred_element_type=jnp.float32)
        return (image_part, window_part)
    image_dir, window_dir = lax.map(per_block, (image_groups, window))
    window_dir = window_dir.reshape(BLOCKS, 3, GROUP, D)
    text_dir = window_dir[:, 1] + jnp.roll(window_dir[:, 0], -1, axis=0) + jnp.roll(window_dir[:, 2], 1, axis=0)
    image_grad = backward_norm(image_unit, image_inverse, image_dir.reshape(PAIRS, D))
    text_grad = backward_norm(text_unit, text_inverse, text_dir.reshape(PAIRS, D))
    return (image_grad, text_grad)
```

```python
import functools

import jax
import jax.numpy as jnp
from jax import lax
from jax.experimental import pallas as pl
from jax.experimental.pallas import tpu as pltpu
from jax.sharding import PartitionSpec as P

PIECES = 2
NT = (((1,), (1,)), ((), ()))
TN = (((0,), (0,)), ((), ()))


def dot(a, b, dims):
    return lax.dot_general(a, b, dims, preferred_element_type=jnp.float32)


def inverse_norm(values):
    return lax.rsqrt(jnp.sum(values * values, axis=-1, keepdims=True) + 1e-06)


def backward_norm(values, inverse, direction):
    unit = values * inverse
    return (direction - unit * jnp.sum(unit * direction, axis=-1, keepdims=True)) * inverse


def kernel(
    groups, rows,
    scale_ref, offset_ref, image_hbm, text_hbm,
    image_out, text_out,
    image_x, text_x, image_inv, text_inv,
    image_low, text_low, coef,
    image_part, text_part,
    image_send, mate_send, ext_send,
    image_recv, mate_recv, ext_recv,
    image_res, text_res,
    load_sem, store_sem, send_sem, recv_sem,
):
    g = lax.axis_index("dp")
    s = lax.axis_index("sub")
    odd = lax.rem(g, 2)
    mate = g + 1 - 2 * odd
    ext = lax.rem(g - 1 + 2 * odd + groups, groups)
    partner = (g, 1 - s)
    mate_id = (mate, s)
    ext_id = (ext, s)

    step = rows // PIECES
    pieces = [pl.ds(c * step, step) for c in range(PIECES)]

    barrier = pltpu.get_barrier_semaphore()
    for who in (partner, mate_id, ext_id):
        pl.semaphore_signal(barrier, inc=1, device_id=who, device_id_type=pl.DeviceIdType.MESH)

    loads = []
    for c, piece in enumerate(pieces):
        pair = (
            pltpu.make_async_copy(text_hbm.at[piece], text_x.at[piece], load_sem.at[0, c]),
            pltpu.make_async_copy(image_hbm.at[piece], image_x.at[piece], load_sem.at[1, c]),
        )
        for copy in pair:
            copy.start()
        loads.append(pair)

    def send(src, dst, kind, c, who):
        copy = pltpu.make_async_remote_copy(
            src_ref=src,
            dst_ref=dst,
            send_sem=send_sem.at[kind, c],
            recv_sem=recv_sem.at[kind, c],
            device_id=who,
            device_id_type=pl.DeviceIdType.MESH,
        )
        copy.start()
        return copy

    ext_text, mate_text, partner_image = [], [], []
    for c, piece in enumerate(pieces):
        loads[c][0].wait()
        values = text_x[piece, :]
        inverse = inverse_norm(values)
        text_inv[piece, :] = inverse
        text_low[piece, :] = (values * inverse).astype(jnp.bfloat16)
        if c == 0:
            pl.semaphore_wait(barrier, 3)
        own = text_low.at[piece]
        ext_text.append(send(own, text_low.at[pl.ds(2 * rows + c * step, step)], 0, c, ext_id))
        mate_text.append(send(own, text_low.at[pl.ds(rows + c * step, step)], 1, c, mate_id))
        loads[c][1].wait()
        values = image_x[piece, :]
        inverse = inverse_norm(values)
        image_inv[piece, :] = inverse
        image_low[piece, :] = (values * inverse).astype(jnp.bfloat16)
        own = image_low.at[piece]
        partner_image.append(send(own, image_low.at[pl.ds(rows + c * step, step)], 2, c, partner))

    scale = scale_ref[0, 0]
    offset = offset_ref[0, 0]

    def fill(text_at, text_rows, image_at, image_rows, diagonal=False):
        texts = pl.ds(text_at, text_rows)
        images = pl.ds(image_at, image_rows)
        scores = scale * dot(text_low[texts, :], image_low[images, :], NT) + offset
        if diagonal:
            row = lax.broadcasted_iota(jnp.int32, scores.shape, 0)
            col = lax.broadcasted_iota(jnp.int32, scores.shape, 1)
            label = jnp.where(row == col, jnp.float32(1.0), jnp.float32(-1.0))
            values = -label * scale * (1.0 / (1.0 + jnp.exp(label * scores)))
        else:
            values = scale * (1.0 / (1.0 + jnp.exp(-scores)))
        coef[texts, images] = values.astype(jnp.bfloat16)

    fill(0, rows, 0, rows, diagonal=True)
    for copy in mate_text:
        copy.wait_recv()
    fill(rows, rows, 0, rows)
    for copy in partner_image:
        copy.wait_recv()
    fill(0, 2 * rows, rows, rows)

    ext_terms, mate_terms, image_terms = [], [], []
    for c, piece in enumerate(pieces):
        ext_text[c].wait_recv()
        at = 2 * rows + c * step
        fill(at, step, 0, 2 * rows)
        terms = jnp.dot(
            coef[pl.ds(at, step), :], image_low[...], preferred_element_type=jnp.float32
        )
        ext_send[piece, :] = terms.astype(jnp.bfloat16)
        ext_terms.append(send(ext_send.at[piece], ext_recv.at[piece], 3, c, ext_id))

    image_send[...] = dot(coef[:, rows:], text_low[...], TN).astype(jnp.bfloat16)
    for c, piece in enumerate(pieces):
        image_terms.append(send(image_send.at[piece], image_recv.at[piece], 5, c, partner))

    mate_send[...] = jnp.dot(
        coef[pl.ds(rows, rows), :], image_low[...], preferred_element_type=jnp.float32
    ).astype(jnp.bfloat16)
    for c, piece in enumerate(pieces):
        mate_terms.append(send(mate_send.at[piece], mate_recv.at[piece], 4, c, mate_id))

    image_part[...] = dot(coef[:, :rows], text_low[...], TN)
    text_part[...] = jnp.dot(
        coef[pl.ds(0, rows), :], image_low[...], preferred_element_type=jnp.float32
    )

    stores = []
    for c, piece in enumerate(pieces):
        mate_terms[c].wait_recv()
        ext_terms[c].wait_recv()
        direction = (
            text_part[piece, :]
            + mate_recv[piece, :].astype(jnp.float32)
            + ext_recv[piece, :].astype(jnp.float32)
        )
        text_res[piece, :] = backward_norm(text_x[piece, :], text_inv[piece, :], direction)
        copy = pltpu.make_async_copy(text_res.at[piece], text_out.at[piece], store_sem.at[0, c])
        copy.start()
        stores.append(copy)

        image_terms[c].wait_recv()
        direction = image_part[piece, :] + image_recv[piece, :].astype(jnp.float32)
        image_res[piece, :] = backward_norm(image_x[piece, :], image_inv[piece, :], direction)
        copy = pltpu.make_async_copy(image_res.at[piece], image_out.at[piece], store_sem.at[1, c])
        copy.start()
        stores.append(copy)

    for copies in (ext_text, mate_text, partner_image, ext_terms, mate_terms, image_terms):
        for copy in copies:
            copy.wait_send()
    for copy in stores:
        copy.wait()


def shards(groups, image, text, scale, offset):
    rows, width = image.shape
    full = functools.partial(pltpu.VMEM)
    f32, low = jnp.float32, jnp.bfloat16
    return pl.pallas_call(
        functools.partial(kernel, groups, rows),
        out_shape=(jax.ShapeDtypeStruct((rows, width), f32),) * 2,
        in_specs=[pl.BlockSpec(memory_space=pltpu.SMEM)] * 2
        + [pl.BlockSpec(memory_space=pl.ANY)] * 2,
        out_specs=(pl.BlockSpec(memory_space=pl.ANY),) * 2,
        scratch_shapes=[
            full((rows, width), f32),
            full((rows, width), f32),
            full((rows, 1), f32),
            full((rows, 1), f32),
            full((2 * rows, width), low),
            full((3 * rows, width), low),
            full((3 * rows, 2 * rows), low),
            full((rows, width), f32),
            full((rows, width), f32),
        ]
        + [full((rows, width), low)] * 6
        + [full((rows, width), f32)] * 2
        + [
            pltpu.SemaphoreType.DMA((2, PIECES)),
            pltpu.SemaphoreType.DMA((2, PIECES)),
            pltpu.SemaphoreType.DMA((6, PIECES)),
            pltpu.SemaphoreType.DMA((6, PIECES)),
        ],
        compiler_params=pltpu.CompilerParams(
            collective_id=0, has_side_effects=True, vmem_limit_bytes=32 * 1024 * 1024
        ),
        cost_estimate=pl.CostEstimate(
            flops=36 * rows * rows * width,
            bytes_accessed=16 * rows * width,
            transcendentals=6 * rows * rows,
        ),
    )(scale.reshape(1, 1), offset.reshape(1, 1), image, text)


def solution(mesh):
    if mesh.shape["sub"] != 2 or mesh.shape["dp"] % 2 or mesh.shape["dp"] < 4:
        raise ValueError("unsupported mesh")
    placed = (P(("dp", "sub"), None), P(("dp", "sub"), None), P(), P())
    return jax.shard_map(
        functools.partial(shards, mesh.shape["dp"]),
        mesh=mesh,
        in_specs=placed,
        out_specs=(P(("dp", "sub"), None), P(("dp", "sub"), None)),
        check_vma=False,
    )
```

```python
import functools

import jax
import jax.numpy as jnp
from jax import lax
from jax.experimental import pallas as pl
from jax.experimental.pallas import tpu as pltpu
from jax.sharding import PartitionSpec as P

PIECES = 4
NT = (((1,), (1,)), ((), ()))
TN = (((0,), (0,)), ((), ()))


def dot(a, b, dims):
    return lax.dot_general(a, b, dims, preferred_element_type=jnp.float32)


def inverse_norm(values):
    return lax.rsqrt(jnp.sum(values * values, axis=-1, keepdims=True) + 1e-06)


def backward_norm(values, inverse, direction):
    unit = values * inverse
    return (direction - unit * jnp.sum(unit * direction, axis=-1, keepdims=True)) * inverse


def kernel(
    groups, rows,
    scale_ref, offset_ref, image_hbm, text_hbm,
    image_out, text_out,
    image_x, text_x, image_inv, text_inv,
    image_low, text_low, coef, partner_coef,
    image_part, text_part,
    image_send, mate_send, ext_send,
    image_recv, mate_recv, ext_recv,
    load_sem, send_sem, recv_sem,
):
    g = lax.axis_index("dp")
    s = lax.axis_index("sub")
    odd = lax.rem(g, 2)
    mate = g + 1 - 2 * odd
    ext = lax.rem(g - 1 + 2 * odd + groups, groups)
    partner = (g, 1 - s)
    mate_id = (mate, s)
    ext_id = (ext, s)

    step = rows // PIECES
    pieces = [pl.ds(c * step, step) for c in range(PIECES)]

    barrier = pltpu.get_barrier_semaphore()
    for who in (partner, mate_id, ext_id):
        pl.semaphore_signal(barrier, inc=1, device_id=who, device_id_type=pl.DeviceIdType.MESH)

    loads = []
    for c, piece in enumerate(pieces):
        pair = (
            pltpu.make_async_copy(text_hbm.at[piece], text_x.at[piece], load_sem.at[0, c]),
            pltpu.make_async_copy(image_hbm.at[piece], image_x.at[piece], load_sem.at[1, c]),
        )
        for copy in pair:
            copy.start()
        loads.append(pair)

    def send(src, dst, kind, c, who):
        copy = pltpu.make_async_remote_copy(
            src_ref=src,
            dst_ref=dst,
            send_sem=send_sem.at[kind, c],
            recv_sem=recv_sem.at[kind, c],
            device_id=who,
            device_id_type=pl.DeviceIdType.MESH,
        )
        copy.start()
        return copy

    ext_text, mate_text, partner_image = [], [], []
    for c, piece in enumerate(pieces):
        loads[c][0].wait()
        values = text_x[piece, :]
        inverse = inverse_norm(values)
        text_inv[piece, :] = inverse
        text_low[piece, :] = (values * inverse).astype(jnp.bfloat16)
        if c == 0:
            pl.semaphore_wait(barrier, 3)
        own = text_low.at[piece]
        ext_text.append(send(own, text_low.at[pl.ds(2 * rows + c * step, step)], 0, c, ext_id))
        mate_text.append(send(own, text_low.at[pl.ds(rows + c * step, step)], 1, c, mate_id))
        loads[c][1].wait()
        values = image_x[piece, :]
        inverse = inverse_norm(values)
        image_inv[piece, :] = inverse
        image_low[piece, :] = (values * inverse).astype(jnp.bfloat16)
        own = image_low.at[piece]
        partner_image.append(send(own, image_low.at[pl.ds(rows + c * step, step)], 2, c, partner))

    scale = scale_ref[0, 0]
    offset = offset_ref[0, 0]

    def fill(text_at, text_rows, image_at, image_rows, diagonal=False):
        texts = pl.ds(text_at, text_rows)
        images = pl.ds(image_at, image_rows)
        scores = scale * dot(text_low[texts, :], image_low[images, :], NT) + offset
        if diagonal:
            row = lax.broadcasted_iota(jnp.int32, scores.shape, 0)
            col = lax.broadcasted_iota(jnp.int32, scores.shape, 1)
            label = jnp.where(row == col, jnp.float32(1.0), jnp.float32(-1.0))
            values = -label * scale * (1.0 / (1.0 + jnp.exp(label * scores)))
        else:
            values = scale * (1.0 / (1.0 + jnp.exp(-scores)))
        coef[texts, images] = values.astype(jnp.bfloat16)

    def terms(texts):
        return jnp.dot(coef[texts, :], image_low[...], preferred_element_type=jnp.float32)

    fill(0, rows, 0, rows, diagonal=True)
    for copy in mate_text:
        copy.wait_recv()
    fill(rows, rows, 0, rows)
    for copy in partner_image:
        copy.wait_recv()
    fill(0, 2 * rows, rows, rows)
    for copy in ext_text:
        copy.wait_recv()
    fill(2 * rows, rows, 0, 2 * rows)
    partner_coef[...] = coef[:, rows:].T

    ext_terms, mate_terms, image_terms = [], [], []
    for c, piece in enumerate(pieces):
        ext_send[piece, :] = terms(pl.ds(2 * rows + c * step, step)).astype(jnp.bfloat16)
        ext_terms.append(send(ext_send.at[piece], ext_recv.at[piece], 3, c, ext_id))
        image_send[piece, :] = jnp.dot(
            partner_coef[piece, :], text_low[...], preferred_element_type=jnp.float32
        ).astype(jnp.bfloat16)
        image_terms.append(send(image_send.at[piece], image_recv.at[piece], 5, c, partner))

    mate_send[...] = terms(pl.ds(rows, rows)).astype(jnp.bfloat16)
    for c, piece in enumerate(pieces):
        mate_terms.append(send(mate_send.at[piece], mate_recv.at[piece], 4, c, mate_id))

    image_part[...] = dot(coef[:, :rows], text_low[...], TN)
    text_part[...] = terms(pl.ds(0, rows))

    for c, piece in enumerate(pieces):
        mate_terms[c].wait_recv()
        ext_terms[c].wait_recv()
        direction = (
            text_part[piece, :]
            + mate_recv[piece, :].astype(jnp.float32)
            + ext_recv[piece, :].astype(jnp.float32)
        )
        text_out[piece, :] = backward_norm(text_x[piece, :], text_inv[piece, :], direction)
        image_terms[c].wait_recv()
        direction = image_part[piece, :] + image_recv[piece, :].astype(jnp.float32)
        image_out[piece, :] = backward_norm(image_x[piece, :], image_inv[piece, :], direction)

    for copies in (ext_text, mate_text, partner_image, ext_terms, mate_terms, image_terms):
        for copy in copies:
            copy.wait_send()


def store(image_ref, text_ref, image_out, text_out, sem):
    copies = [
        pltpu.make_async_copy(image_ref, image_out, sem.at[0]),
        pltpu.make_async_copy(text_ref, text_out, sem.at[1]),
    ]
    for copy in copies:
        copy.start()
    for copy in copies:
        copy.wait()


def shards(groups, image, text, scale, offset):
    rows, width = image.shape
    full = pltpu.VMEM
    f32, low = jnp.float32, jnp.bfloat16
    image = pltpu.with_memory_space_constraint(image, pltpu.HBM)
    text = pltpu.with_memory_space_constraint(text, pltpu.HBM)
    grads = pl.pallas_call(
        functools.partial(kernel, groups, rows),
        out_shape=(jax.ShapeDtypeStruct((rows, width), f32),) * 2,
        in_specs=[pl.BlockSpec(memory_space=pltpu.SMEM)] * 2
        + [pl.BlockSpec(memory_space=pltpu.HBM)] * 2,
        out_specs=(pl.BlockSpec(memory_space=pltpu.VMEM),) * 2,
        scratch_shapes=[
            full((rows, width), f32),
            full((rows, width), f32),
            full((rows, 1), f32),
            full((rows, 1), f32),
            full((2 * rows, width), low),
            full((3 * rows, width), low),
            full((3 * rows, 2 * rows), low),
            full((rows, 3 * rows), low),
            full((rows, width), f32),
            full((rows, width), f32),
        ]
        + [full((rows, width), low)] * 6
        + [
            pltpu.SemaphoreType.DMA((2, PIECES)),
            pltpu.SemaphoreType.DMA((6, PIECES)),
            pltpu.SemaphoreType.DMA((6, PIECES)),
        ],
        compiler_params=pltpu.CompilerParams(
            collective_id=0, has_side_effects=True, vmem_limit_bytes=32 * 1024 * 1024
        ),
        cost_estimate=pl.CostEstimate(
            flops=36 * rows * rows * width,
            bytes_accessed=16 * rows * width,
            transcendentals=6 * rows * rows,
        ),
    )(scale.reshape(1, 1), offset.reshape(1, 1), image, text)
    return tuple(
        pl.pallas_call(
            store,
            out_shape=(jax.ShapeDtypeStruct((rows, width), f32),) * 2,
            in_specs=[pl.BlockSpec(memory_space=pl.ANY)] * 2,
            out_specs=(pl.BlockSpec(memory_space=pltpu.HBM),) * 2,
            scratch_shapes=[pltpu.SemaphoreType.DMA((2,))],
            compiler_params=pltpu.CompilerParams(vmem_limit_bytes=16 * 1024 * 1024),
        )(*grads)
    )


def solution(mesh):
    if mesh.shape["sub"] != 2 or mesh.shape["dp"] % 2 or mesh.shape["dp"] < 4:
        raise ValueError("unsupported mesh")
    placed = (P(("dp", "sub"), None), P(("dp", "sub"), None), P(), P())
    return jax.shard_map(
        functools.partial(shards, mesh.shape["dp"]),
        mesh=mesh,
        in_specs=placed,
        out_specs=(P(("dp", "sub"), None), P(("dp", "sub"), None)),
        check_vma=False,
    )
```

```python
import functools

import jax
import jax.numpy as jnp
from jax import lax
from jax.experimental import pallas as pl
from jax.experimental.pallas import tpu as pltpu
from jax.sharding import PartitionSpec as P

PIECES = 4
EARLY = 3
NT = (((1,), (1,)), ((), ()))
TN = (((0,), (0,)), ((), ()))


def dot(a, b, dims):
    return lax.dot_general(a, b, dims, preferred_element_type=jnp.float32)


def inverse_norm(values):
    return lax.rsqrt(jnp.sum(values * values, axis=-1, keepdims=True) + 1e-06)


def backward_norm(values, inverse, direction):
    unit = values * inverse
    return (direction - unit * jnp.sum(unit * direction, axis=-1, keepdims=True)) * inverse


def kernel(
    groups, rows,
    scale_ref, offset_ref, image_hbm, text_hbm,
    image_out, text_out,
    image_x, text_x, image_inv, text_inv,
    image_low, text_low, coef, partner_coef,
    image_part, text_part,
    image_send, mate_send, ext_send,
    image_recv, mate_recv, ext_recv,
    load_sem, send_sem, recv_sem, turn,
):
    g = lax.axis_index("dp")
    s = lax.axis_index("sub")
    odd = lax.rem(g, 2)
    mate = g + 1 - 2 * odd
    ext = lax.rem(g - 1 + 2 * odd + groups, groups)
    partner = (g, 1 - s)
    mate_id = (mate, s)
    ext_id = (ext, s)

    leads = lax.rem((g + 1) // 2, 2) == 1

    step = rows // PIECES
    pieces = [pl.ds(c * step, step) for c in range(PIECES)]

    barrier = pltpu.get_barrier_semaphore()
    for who in (partner, mate_id, ext_id):
        pl.semaphore_signal(barrier, inc=1, device_id=who, device_id_type=pl.DeviceIdType.MESH)

    loads = []
    for c, piece in enumerate(pieces):
        pair = (
            pltpu.make_async_copy(text_hbm.at[piece], text_x.at[piece], load_sem.at[0, c]),
            pltpu.make_async_copy(image_hbm.at[piece], image_x.at[piece], load_sem.at[1, c]),
        )
        for copy in pair:
            copy.start()
        loads.append(pair)

    def remote(src, dst, kind, c, who):
        return pltpu.make_async_remote_copy(
            src_ref=src,
            dst_ref=dst,
            send_sem=send_sem.at[kind, c],
            recv_sem=recv_sem.at[kind, c],
            device_id=who,
            device_id_type=pl.DeviceIdType.MESH,
        )

    def send(*args):
        copy = remote(*args)
        copy.start()
        return copy

    ext_text, mate_text, partner_image = [], [], []
    for c, piece in enumerate(pieces):
        loads[c][0].wait()
        values = text_x[piece, :]
        inverse = inverse_norm(values)
        text_inv[piece, :] = inverse
        text_low[piece, :] = (values * inverse).astype(jnp.bfloat16)
        if c == 0:
            pl.semaphore_wait(barrier, 3)
        own = text_low.at[piece]
        ext_text.append(remote(own, text_low.at[pl.ds(2 * rows + c * step, step)], 0, c, ext_id))
        pl.when(leads)(ext_text[c].start)
        mate_text.append(send(own, text_low.at[pl.ds(rows + c * step, step)], 1, c, mate_id))
        loads[c][1].wait()
        values = image_x[piece, :]
        inverse = inverse_norm(values)
        image_inv[piece, :] = inverse
        image_low[piece, :] = (values * inverse).astype(jnp.bfloat16)
        own = image_low.at[piece]
        partner_image.append(remote(own, image_low.at[pl.ds(rows + c * step, step)], 2, c, partner))
        pl.when(leads)(partner_image[c].start)

    scale = scale_ref[0, 0]
    offset = offset_ref[0, 0]

    def fill(text_at, text_rows, image_at, image_rows, diagonal=False):
        texts = pl.ds(text_at, text_rows)
        images = pl.ds(image_at, image_rows)
        scores = scale * dot(text_low[texts, :], image_low[images, :], NT) + offset
        if diagonal:
            row = lax.broadcasted_iota(jnp.int32, scores.shape, 0)
            col = lax.broadcasted_iota(jnp.int32, scores.shape, 1)
            label = jnp.where(row == col, jnp.float32(1.0), jnp.float32(-1.0))
            values = -label * scale * (1.0 / (1.0 + jnp.exp(label * scores)))
        else:
            values = scale * (1.0 / (1.0 + jnp.exp(-scores)))
        coef[texts, images] = values.astype(jnp.bfloat16)

    def terms(texts):
        return jnp.dot(coef[texts, :], image_low[...], preferred_element_type=jnp.float32)

    fill(0, rows, 0, rows, diagonal=True)

    @pl.when(leads)
    def _():
        for c in range(EARLY):
            ext_text[c].wait_send()
            partner_image[c].wait_send()
        pl.semaphore_signal(
            turn, inc=1, device_id=mate_id, device_id_type=pl.DeviceIdType.MESH
        )

    @pl.when(jnp.logical_not(leads))
    def _():
        pl.semaphore_wait(turn, 1)
        for c in range(PIECES):
            ext_text[c].start()
            partner_image[c].start()

    for copy in mate_text:
        copy.wait_recv()
    fill(rows, rows, 0, rows)
    for copy in partner_image:
        copy.wait_recv()
    fill(0, 2 * rows, rows, rows)
    for copy in ext_text:
        copy.wait_recv()
    fill(2 * rows, rows, 0, 2 * rows)
    partner_coef[...] = coef[:, rows:].T

    ext_terms, mate_terms, image_terms = [], [], []
    for c, piece in enumerate(pieces):
        ext_send[piece, :] = terms(pl.ds(2 * rows + c * step, step)).astype(jnp.bfloat16)
        ext_terms.append(send(ext_send.at[piece], ext_recv.at[piece], 3, c, ext_id))
        image_send[piece, :] = jnp.dot(
            partner_coef[piece, :], text_low[...], preferred_element_type=jnp.float32
        ).astype(jnp.bfloat16)
        image_terms.append(send(image_send.at[piece], image_recv.at[piece], 5, c, partner))

    mate_send[...] = terms(pl.ds(rows, rows)).astype(jnp.bfloat16)
    for c, piece in enumerate(pieces):
        mate_terms.append(send(mate_send.at[piece], mate_recv.at[piece], 4, c, mate_id))

    image_part[...] = dot(coef[:, :rows], text_low[...], TN)
    text_part[...] = terms(pl.ds(0, rows))

    for c, piece in enumerate(pieces):
        mate_terms[c].wait_recv()
        ext_terms[c].wait_recv()
        direction = (
            text_part[piece, :]
            + mate_recv[piece, :].astype(jnp.float32)
            + ext_recv[piece, :].astype(jnp.float32)
        )
        text_out[piece, :] = backward_norm(text_x[piece, :], text_inv[piece, :], direction)
        image_terms[c].wait_recv()
        direction = image_part[piece, :] + image_recv[piece, :].astype(jnp.float32)
        image_out[piece, :] = backward_norm(image_x[piece, :], image_inv[piece, :], direction)

    @pl.when(jnp.logical_not(leads))
    def _():
        for c in range(EARLY):
            ext_text[c].wait_send()
            partner_image[c].wait_send()

    for copies in (
        ext_text[EARLY:], partner_image[EARLY:], mate_text, ext_terms, mate_terms, image_terms
    ):
        for copy in copies:
            copy.wait_send()


def store(image_ref, text_ref, image_out, text_out, sem):
    copies = [
        pltpu.make_async_copy(image_ref, image_out, sem.at[0]),
        pltpu.make_async_copy(text_ref, text_out, sem.at[1]),
    ]
    for copy in copies:
        copy.start()
    for copy in copies:
        copy.wait()


def shards(groups, image, text, scale, offset):
    rows, width = image.shape
    full = pltpu.VMEM
    f32, low = jnp.float32, jnp.bfloat16
    image = pltpu.with_memory_space_constraint(image, pltpu.HBM)
    text = pltpu.with_memory_space_constraint(text, pltpu.HBM)
    grads = pl.pallas_call(
        functools.partial(kernel, groups, rows),
        out_shape=(jax.ShapeDtypeStruct((rows, width), f32),) * 2,
        in_specs=[pl.BlockSpec(memory_space=pltpu.SMEM)] * 2
        + [pl.BlockSpec(memory_space=pltpu.HBM)] * 2,
        out_specs=(pl.BlockSpec(memory_space=pltpu.VMEM),) * 2,
        scratch_shapes=[
            full((rows, width), f32),
            full((rows, width), f32),
            full((rows, 1), f32),
            full((rows, 1), f32),
            full((2 * rows, width), low),
            full((3 * rows, width), low),
            full((3 * rows, 2 * rows), low),
            full((rows, 3 * rows), low),
            full((rows, width), f32),
            full((rows, width), f32),
        ]
        + [full((rows, width), low)] * 6
        + [
            pltpu.SemaphoreType.DMA((2, PIECES)),
            pltpu.SemaphoreType.DMA((6, PIECES)),
            pltpu.SemaphoreType.DMA((6, PIECES)),
            pltpu.SemaphoreType.REGULAR,
        ],
        compiler_params=pltpu.CompilerParams(
            collective_id=0, has_side_effects=True, vmem_limit_bytes=32 * 1024 * 1024
        ),
        cost_estimate=pl.CostEstimate(
            flops=36 * rows * rows * width,
            bytes_accessed=16 * rows * width,
            transcendentals=6 * rows * rows,
        ),
    )(scale.reshape(1, 1), offset.reshape(1, 1), image, text)
    return tuple(
        pl.pallas_call(
            store,
            out_shape=(jax.ShapeDtypeStruct((rows, width), f32),) * 2,
            in_specs=[pl.BlockSpec(memory_space=pl.ANY)] * 2,
            out_specs=(pl.BlockSpec(memory_space=pltpu.HBM),) * 2,
            scratch_shapes=[pltpu.SemaphoreType.DMA((2,))],
            compiler_params=pltpu.CompilerParams(vmem_limit_bytes=16 * 1024 * 1024),
        )(*grads)
    )


def solution(mesh):
    if mesh.shape["sub"] != 2 or mesh.shape["dp"] % 4 or mesh.shape["dp"] < 4:
        raise ValueError("unsupported mesh")
    placed = (P(("dp", "sub"), None), P(("dp", "sub"), None), P(), P())
    return jax.shard_map(
        functools.partial(shards, mesh.shape["dp"]),
        mesh=mesh,
        in_specs=placed,
        out_specs=(P(("dp", "sub"), None), P(("dp", "sub"), None)),
        check_vma=False,
    )
```

```python
import functools

import jax
import jax.numpy as jnp
from jax import lax
from jax.experimental import pallas as pl
from jax.experimental.pallas import tpu as pltpu
from jax.sharding import PartitionSpec as P

PIECES = 4
EARLY = 3
NT = (((1,), (1,)), ((), ()))
TN = (((0,), (0,)), ((), ()))


def dot(a, b, dims):
    return lax.dot_general(a, b, dims, preferred_element_type=jnp.float32)


def inverse_norm(values):
    return lax.rsqrt(jnp.sum(values * values, axis=-1, keepdims=True) + 1e-06)


def backward_norm(values, inverse, direction):
    unit = values * inverse
    return (direction - unit * jnp.sum(unit * direction, axis=-1, keepdims=True)) * inverse


def kernel(
    groups, rows,
    scale_ref, offset_ref, image_hbm, text_hbm,
    image_out, text_out,
    image_x, text_x, image_inv, text_inv,
    image_low, text_low, coef, partner_coef,
    image_part, text_part,
    image_send, mate_send, ext_send,
    image_recv, mate_recv, ext_recv,
    load_sem, send_sem, recv_sem, turn,
):
    g = lax.axis_index("dp")
    s = lax.axis_index("sub")
    odd = lax.rem(g, 2)
    mate = g + 1 - 2 * odd
    ext = lax.rem(g - 1 + 2 * odd + groups, groups)
    partner = (g, 1 - s)
    mate_id = (mate, s)
    ext_id = (ext, s)

    leads = lax.rem((g + 1) // 2, 2) == 0

    step = rows // PIECES
    pieces = [pl.ds(c * step, step) for c in range(PIECES)]

    barrier = pltpu.get_barrier_semaphore()
    for who in (partner, mate_id, ext_id):
        pl.semaphore_signal(barrier, inc=1, device_id=who, device_id_type=pl.DeviceIdType.MESH)

    loads = []
    for c, piece in enumerate(pieces):
        pair = (
            pltpu.make_async_copy(text_hbm.at[piece], text_x.at[piece], load_sem.at[0, c]),
            pltpu.make_async_copy(image_hbm.at[piece], image_x.at[piece], load_sem.at[1, c]),
        )
        for copy in pair:
            copy.start()
        loads.append(pair)

    def remote(src, dst, kind, c, who):
        return pltpu.make_async_remote_copy(
            src_ref=src,
            dst_ref=dst,
            send_sem=send_sem.at[kind, c],
            recv_sem=recv_sem.at[kind, c],
            device_id=who,
            device_id_type=pl.DeviceIdType.MESH,
        )

    def send(*args):
        copy = remote(*args)
        copy.start()
        return copy

    ext_text, mate_text, partner_image = [], [], []
    for c, piece in enumerate(pieces):
        loads[c][0].wait()
        values = text_x[piece, :]
        inverse = inverse_norm(values)
        text_inv[piece, :] = inverse
        text_low[piece, :] = (values * inverse).astype(jnp.bfloat16)
        if c == 0:
            pl.semaphore_wait(barrier, 3)
        own = text_low.at[piece]
        ext_text.append(remote(own, text_low.at[pl.ds(2 * rows + c * step, step)], 0, c, ext_id))
        pl.when(leads)(ext_text[c].start)
        mate_text.append(send(own, text_low.at[pl.ds(rows + c * step, step)], 1, c, mate_id))
        loads[c][1].wait()
        values = image_x[piece, :]
        inverse = inverse_norm(values)
        image_inv[piece, :] = inverse
        image_low[piece, :] = (values * inverse).astype(jnp.bfloat16)
        own = image_low.at[piece]
        partner_image.append(remote(own, image_low.at[pl.ds(rows + c * step, step)], 2, c, partner))
        pl.when(leads)(partner_image[c].start)

    scale = scale_ref[0, 0]
    offset = offset_ref[0, 0]

    def fill(text_at, text_rows, image_at, image_rows, diagonal=False):
        texts = pl.ds(text_at, text_rows)
        images = pl.ds(image_at, image_rows)
        scores = scale * dot(text_low[texts, :], image_low[images, :], NT) + offset
        if diagonal:
            row = lax.broadcasted_iota(jnp.int32, scores.shape, 0)
            col = lax.broadcasted_iota(jnp.int32, scores.shape, 1)
            label = jnp.where(row == col, jnp.float32(1.0), jnp.float32(-1.0))
            values = -label * scale * (1.0 / (1.0 + jnp.exp(label * scores)))
        else:
            values = scale * (1.0 / (1.0 + jnp.exp(-scores)))
        coef[texts, images] = values.astype(jnp.bfloat16)

    def terms(texts):
        return jnp.dot(coef[texts, :], image_low[...], preferred_element_type=jnp.float32)

    fill(0, rows, 0, rows, diagonal=True)

    @pl.when(leads)
    def _():
        for c in range(EARLY):
            ext_text[c].wait_send()
            partner_image[c].wait_send()
        pl.semaphore_signal(
            turn, inc=1, device_id=mate_id, device_id_type=pl.DeviceIdType.MESH
        )

    @pl.when(jnp.logical_not(leads))
    def _():
        pl.semaphore_wait(turn, 1)
        for c in range(PIECES):
            ext_text[c].start()
            partner_image[c].start()

    for copy in mate_text:
        copy.wait_recv()
    fill(rows, rows, 0, rows)
    for copy in partner_image:
        copy.wait_recv()
    fill(0, 2 * rows, rows, rows)
    for copy in ext_text:
        copy.wait_recv()
    fill(2 * rows, rows, 0, 2 * rows)
    partner_coef[...] = coef[:, rows:].T

    ext_terms, mate_terms, image_terms = [], [], []
    for c, piece in enumerate(pieces):
        ext_send[piece, :] = terms(pl.ds(2 * rows + c * step, step)).astype(jnp.bfloat16)
        ext_terms.append(send(ext_send.at[piece], ext_recv.at[piece], 3, c, ext_id))
        image_send[piece, :] = jnp.dot(
            partner_coef[piece, :], text_low[...], preferred_element_type=jnp.float32
        ).astype(jnp.bfloat16)
        image_terms.append(send(image_send.at[piece], image_recv.at[piece], 5, c, partner))

    mate_send[...] = terms(pl.ds(rows, rows)).astype(jnp.bfloat16)
    for c, piece in enumerate(pieces):
        mate_terms.append(send(mate_send.at[piece], mate_recv.at[piece], 4, c, mate_id))

    image_part[...] = dot(coef[:, :rows], text_low[...], TN)
    text_part[...] = terms(pl.ds(0, rows))

    for c, piece in enumerate(pieces):
        mate_terms[c].wait_recv()
        ext_terms[c].wait_recv()
        direction = (
            text_part[piece, :]
            + mate_recv[piece, :].astype(jnp.float32)
            + ext_recv[piece, :].astype(jnp.float32)
        )
        text_out[piece, :] = backward_norm(text_x[piece, :], text_inv[piece, :], direction)
        image_terms[c].wait_recv()
        direction = image_part[piece, :] + image_recv[piece, :].astype(jnp.float32)
        image_out[piece, :] = backward_norm(image_x[piece, :], image_inv[piece, :], direction)

    @pl.when(jnp.logical_not(leads))
    def _():
        for c in range(EARLY):
            ext_text[c].wait_send()
            partner_image[c].wait_send()

    for copies in (
        ext_text[EARLY:], partner_image[EARLY:], mate_text, ext_terms, mate_terms, image_terms
    ):
        for copy in copies:
            copy.wait_send()


def store(image_ref, text_ref, image_out, text_out, sem):
    copies = [
        pltpu.make_async_copy(image_ref, image_out, sem.at[0]),
        pltpu.make_async_copy(text_ref, text_out, sem.at[1]),
    ]
    for copy in copies:
        copy.start()
    for copy in copies:
        copy.wait()


def shards(groups, image, text, scale, offset):
    rows, width = image.shape
    full = pltpu.VMEM
    f32, low = jnp.float32, jnp.bfloat16
    image = pltpu.with_memory_space_constraint(image, pltpu.HBM)
    text = pltpu.with_memory_space_constraint(text, pltpu.HBM)
    grads = pl.pallas_call(
        functools.partial(kernel, groups, rows),
        out_shape=(jax.ShapeDtypeStruct((rows, width), f32),) * 2,
        in_specs=[pl.BlockSpec(memory_space=pltpu.SMEM)] * 2
        + [pl.BlockSpec(memory_space=pltpu.HBM)] * 2,
        out_specs=(pl.BlockSpec(memory_space=pltpu.VMEM),) * 2,
        scratch_shapes=[
            full((rows, width), f32),
            full((rows, width), f32),
            full((rows, 1), f32),
            full((rows, 1), f32),
            full((2 * rows, width), low),
            full((3 * rows, width), low),
            full((3 * rows, 2 * rows), low),
            full((rows, 3 * rows), low),
            full((rows, width), f32),
            full((rows, width), f32),
        ]
        + [full((rows, width), low)] * 6
        + [
            pltpu.SemaphoreType.DMA((2, PIECES)),
            pltpu.SemaphoreType.DMA((6, PIECES)),
            pltpu.SemaphoreType.DMA((6, PIECES)),
            pltpu.SemaphoreType.REGULAR,
        ],
        compiler_params=pltpu.CompilerParams(
            collective_id=0, has_side_effects=True, vmem_limit_bytes=32 * 1024 * 1024
        ),
        cost_estimate=pl.CostEstimate(
            flops=36 * rows * rows * width,
            bytes_accessed=16 * rows * width,
            transcendentals=6 * rows * rows,
        ),
    )(scale.reshape(1, 1), offset.reshape(1, 1), image, text)
    return tuple(
        pl.pallas_call(
            store,
            out_shape=(jax.ShapeDtypeStruct((rows, width), f32),) * 2,
            in_specs=[pl.BlockSpec(memory_space=pl.ANY)] * 2,
            out_specs=(pl.BlockSpec(memory_space=pltpu.HBM),) * 2,
            scratch_shapes=[pltpu.SemaphoreType.DMA((2,))],
            compiler_params=pltpu.CompilerParams(vmem_limit_bytes=16 * 1024 * 1024),
        )(*grads)
    )


def solution(mesh):
    if mesh.shape["sub"] != 2 or mesh.shape["dp"] % 4 or mesh.shape["dp"] < 4:
        raise ValueError("unsupported mesh")
    placed = (P(("dp", "sub"), None), P(("dp", "sub"), None), P(), P())
    return jax.shard_map(
        functools.partial(shards, mesh.shape["dp"]),
        mesh=mesh,
        in_specs=placed,
        out_specs=(P(("dp", "sub"), None), P(("dp", "sub"), None)),
        check_vma=False,
    )
```

```python
import functools

import jax
import jax.numpy as jnp
from jax import lax
from jax.experimental import pallas as pl
from jax.experimental.pallas import tpu as pltpu
from jax.sharding import PartitionSpec as P

PIECES = 4
EARLY = 3
NT = (((1,), (1,)), ((), ()))
TN = (((0,), (0,)), ((), ()))


def dot(a, b, dims):
    return lax.dot_general(a, b, dims, preferred_element_type=jnp.float32)


def inverse_norm(values):
    return lax.rsqrt(jnp.sum(values * values, axis=-1, keepdims=True) + 1e-06)


def backward_norm(values, inverse, direction):
    unit = values * inverse
    return (direction - unit * jnp.sum(unit * direction, axis=-1, keepdims=True)) * inverse


def kernel(
    groups, rows,
    scale_ref, offset_ref, image_hbm, text_hbm,
    image_out, text_out,
    image_x, text_x, image_inv, text_inv,
    image_low, text_low, coef, partner_coef,
    image_part, text_part,
    image_send, mate_send, ext_send,
    image_recv, mate_recv, ext_recv,
    load_sem, send_sem, recv_sem, turn,
):
    g = lax.axis_index("dp")
    s = lax.axis_index("sub")
    odd = lax.rem(g, 2)
    mate = g + 1 - 2 * odd
    ext = lax.rem(g - 1 + 2 * odd + groups, groups)
    partner = (g, 1 - s)
    mate_id = (mate, s)
    ext_id = (ext, s)

    wrap = jnp.logical_or(g == 0, g == groups - 1)
    near = jnp.logical_and(lax.rem((g + 1) // 2, 2) == 1, g != groups - 2)
    leads = jnp.logical_or(near, wrap)
    hands_over = jnp.logical_and(leads, g > 1)

    step = rows // PIECES
    pieces = [pl.ds(c * step, step) for c in range(PIECES)]

    barrier = pltpu.get_barrier_semaphore()
    for who in (partner, mate_id, ext_id):
        pl.semaphore_signal(barrier, inc=1, device_id=who, device_id_type=pl.DeviceIdType.MESH)

    loads = []
    for c, piece in enumerate(pieces):
        pair = (
            pltpu.make_async_copy(text_hbm.at[piece], text_x.at[piece], load_sem.at[0, c]),
            pltpu.make_async_copy(image_hbm.at[piece], image_x.at[piece], load_sem.at[1, c]),
        )
        for copy in pair:
            copy.start()
        loads.append(pair)

    def remote(src, dst, kind, c, who):
        return pltpu.make_async_remote_copy(
            src_ref=src,
            dst_ref=dst,
            send_sem=send_sem.at[kind, c],
            recv_sem=recv_sem.at[kind, c],
            device_id=who,
            device_id_type=pl.DeviceIdType.MESH,
        )

    def send(*args):
        copy = remote(*args)
        copy.start()
        return copy

    ext_text, mate_text, partner_image = [], [], []
    for c, piece in enumerate(pieces):
        loads[c][0].wait()
        values = text_x[piece, :]
        inverse = inverse_norm(values)
        text_inv[piece, :] = inverse
        text_low[piece, :] = (values * inverse).astype(jnp.bfloat16)
        if c == 0:
            pl.semaphore_wait(barrier, 3)
        own = text_low.at[piece]
        ext_text.append(remote(own, text_low.at[pl.ds(2 * rows + c * step, step)], 0, c, ext_id))
        pl.when(leads)(ext_text[c].start)
        mate_text.append(send(own, text_low.at[pl.ds(rows + c * step, step)], 1, c, mate_id))
        loads[c][1].wait()
        values = image_x[piece, :]
        inverse = inverse_norm(values)
        image_inv[piece, :] = inverse
        image_low[piece, :] = (values * inverse).astype(jnp.bfloat16)
        own = image_low.at[piece]
        partner_image.append(remote(own, image_low.at[pl.ds(rows + c * step, step)], 2, c, partner))
        pl.when(leads)(partner_image[c].start)

    scale = scale_ref[0, 0]
    offset = offset_ref[0, 0]

    def fill(text_at, text_rows, image_at, image_rows, diagonal=False):
        texts = pl.ds(text_at, text_rows)
        images = pl.ds(image_at, image_rows)
        scores = scale * dot(text_low[texts, :], image_low[images, :], NT) + offset
        if diagonal:
            row = lax.broadcasted_iota(jnp.int32, scores.shape, 0)
            col = lax.broadcasted_iota(jnp.int32, scores.shape, 1)
            label = jnp.where(row == col, jnp.float32(1.0), jnp.float32(-1.0))
            values = -label * scale * (1.0 / (1.0 + jnp.exp(label * scores)))
        else:
            values = scale * (1.0 / (1.0 + jnp.exp(-scores)))
        coef[texts, images] = values.astype(jnp.bfloat16)

    def terms(texts):
        return jnp.dot(coef[texts, :], image_low[...], preferred_element_type=jnp.float32)

    fill(0, rows, 0, rows, diagonal=True)

    @pl.when(hands_over)
    def _():
        for c in range(EARLY):
            ext_text[c].wait_send()
            partner_image[c].wait_send()
        pl.semaphore_signal(
            turn, inc=1, device_id=mate_id, device_id_type=pl.DeviceIdType.MESH
        )

    @pl.when(jnp.logical_not(leads))
    def _():
        pl.semaphore_wait(turn, 1)
        for c in range(PIECES):
            ext_text[c].start()
            partner_image[c].start()

    for copy in mate_text:
        copy.wait_recv()
    fill(rows, rows, 0, rows)
    for copy in partner_image:
        copy.wait_recv()
    fill(0, 2 * rows, rows, rows)
    for copy in ext_text:
        copy.wait_recv()
    fill(2 * rows, rows, 0, 2 * rows)
    partner_coef[...] = coef[:, rows:].T

    ext_terms, mate_terms, image_terms = [], [], []
    for c, piece in enumerate(pieces):
        ext_send[piece, :] = terms(pl.ds(2 * rows + c * step, step)).astype(jnp.bfloat16)
        ext_terms.append(send(ext_send.at[piece], ext_recv.at[piece], 3, c, ext_id))
        image_send[piece, :] = jnp.dot(
            partner_coef[piece, :], text_low[...], preferred_element_type=jnp.float32
        ).astype(jnp.bfloat16)
        image_terms.append(send(image_send.at[piece], image_recv.at[piece], 5, c, partner))

    mate_send[...] = terms(pl.ds(rows, rows)).astype(jnp.bfloat16)
    for c, piece in enumerate(pieces):
        mate_terms.append(send(mate_send.at[piece], mate_recv.at[piece], 4, c, mate_id))

    image_part[...] = dot(coef[:, :rows], text_low[...], TN)
    text_part[...] = terms(pl.ds(0, rows))

    for c, piece in enumerate(pieces):
        mate_terms[c].wait_recv()
        ext_terms[c].wait_recv()
        direction = (
            text_part[piece, :]
            + mate_recv[piece, :].astype(jnp.float32)
            + ext_recv[piece, :].astype(jnp.float32)
        )
        text_out[piece, :] = backward_norm(text_x[piece, :], text_inv[piece, :], direction)
        image_terms[c].wait_recv()
        direction = image_part[piece, :] + image_recv[piece, :].astype(jnp.float32)
        image_out[piece, :] = backward_norm(image_x[piece, :], image_inv[piece, :], direction)

    @pl.when(jnp.logical_not(hands_over))
    def _():
        for c in range(EARLY):
            ext_text[c].wait_send()
            partner_image[c].wait_send()

    for copies in (
        ext_text[EARLY:], partner_image[EARLY:], mate_text, ext_terms, mate_terms, image_terms
    ):
        for copy in copies:
            copy.wait_send()


def store(image_ref, text_ref, image_out, text_out, sem):
    step = image_ref.shape[0] // PIECES
    copies = []
    for c in range(PIECES):
        piece = pl.ds(c * step, step)
        copies += [
            pltpu.make_async_copy(image_ref.at[piece], image_out.at[piece], sem.at[0, c]),
            pltpu.make_async_copy(text_ref.at[piece], text_out.at[piece], sem.at[1, c]),
        ]
    for copy in copies:
        copy.start()
    for copy in copies:
        copy.wait()


def shards(groups, image, text, scale, offset):
    rows, width = image.shape
    full = pltpu.VMEM
    f32, low = jnp.float32, jnp.bfloat16
    image = pltpu.with_memory_space_constraint(image, pltpu.HBM)
    text = pltpu.with_memory_space_constraint(text, pltpu.HBM)
    grads = pl.pallas_call(
        functools.partial(kernel, groups, rows),
        out_shape=(jax.ShapeDtypeStruct((rows, width), f32),) * 2,
        in_specs=[pl.BlockSpec(memory_space=pltpu.SMEM)] * 2
        + [pl.BlockSpec(memory_space=pltpu.HBM)] * 2,
        out_specs=(pl.BlockSpec(memory_space=pltpu.VMEM),) * 2,
        scratch_shapes=[
            full((rows, width), f32),
            full((rows, width), f32),
            full((rows, 1), f32),
            full((rows, 1), f32),
            full((2 * rows, width), low),
            full((3 * rows, width), low),
            full((3 * rows, 2 * rows), low),
            full((rows, 3 * rows), low),
            full((rows, width), f32),
            full((rows, width), f32),
        ]
        + [full((rows, width), low)] * 6
        + [
            pltpu.SemaphoreType.DMA((2, PIECES)),
            pltpu.SemaphoreType.DMA((6, PIECES)),
            pltpu.SemaphoreType.DMA((6, PIECES)),
            pltpu.SemaphoreType.REGULAR,
        ],
        compiler_params=pltpu.CompilerParams(
            collective_id=0, has_side_effects=True, vmem_limit_bytes=32 * 1024 * 1024
        ),
        cost_estimate=pl.CostEstimate(
            flops=36 * rows * rows * width,
            bytes_accessed=16 * rows * width,
            transcendentals=6 * rows * rows,
        ),
    )(scale.reshape(1, 1), offset.reshape(1, 1), image, text)
    return tuple(
        pl.pallas_call(
            store,
            out_shape=(jax.ShapeDtypeStruct((rows, width), f32),) * 2,
            in_specs=[pl.BlockSpec(memory_space=pl.ANY)] * 2,
            out_specs=(pl.BlockSpec(memory_space=pltpu.HBM),) * 2,
            scratch_shapes=[pltpu.SemaphoreType.DMA((2, PIECES))],
            compiler_params=pltpu.CompilerParams(vmem_limit_bytes=16 * 1024 * 1024),
        )(*grads)
    )


def solution(mesh):
    if mesh.shape["sub"] != 2 or mesh.shape["dp"] % 4 or mesh.shape["dp"] < 4:
        raise ValueError("unsupported mesh")
    placed = (P(("dp", "sub"), None), P(("dp", "sub"), None), P(), P())
    return jax.shard_map(
        functools.partial(shards, mesh.shape["dp"]),
        mesh=mesh,
        in_specs=placed,
        out_specs=(P(("dp", "sub"), None), P(("dp", "sub"), None)),
        check_vma=False,
    )
```

```python
import functools

import jax
import jax.numpy as jnp
from jax import lax
from jax.experimental import pallas as pl
from jax.experimental.pallas import tpu as pltpu
from jax.sharding import PartitionSpec as P

PIECES = 4
EARLY = 3
NT = (((1,), (1,)), ((), ()))
TN = (((0,), (0,)), ((), ()))


def dot(a, b, dims):
    return lax.dot_general(a, b, dims, preferred_element_type=jnp.float32)


def inverse_norm(values):
    return lax.rsqrt(jnp.sum(values * values, axis=-1, keepdims=True) + 1e-06)


def backward_norm(values, inverse, direction):
    unit = values * inverse
    return (direction - unit * jnp.sum(unit * direction, axis=-1, keepdims=True)) * inverse


def kernel(
    groups, rows,
    scale_ref, offset_ref, image_hbm, text_hbm,
    image_out, text_out,
    image_x, text_x, image_inv, text_inv,
    image_low, text_low, coef, partner_coef,
    image_part, text_part,
    image_send, mate_send, ext_send,
    image_recv, mate_recv, ext_recv,
    load_sem, send_sem, recv_sem, turn,
):
    g = lax.axis_index("dp")
    s = lax.axis_index("sub")
    odd = lax.rem(g, 2)
    mate = g + 1 - 2 * odd
    ext = lax.rem(g - 1 + 2 * odd + groups, groups)
    partner = (g, 1 - s)
    mate_id = (mate, s)
    ext_id = (ext, s)

    wrap = jnp.logical_or(g == 0, g == groups - 1)
    near = jnp.logical_and(lax.rem((g + 1) // 2, 2) == 1, g != groups - 2)
    leads = jnp.logical_or(near, wrap)
    hands_over = jnp.logical_and(leads, g > 1)

    step = rows // PIECES
    pieces = [pl.ds(c * step, step) for c in range(PIECES)]

    barrier = pltpu.get_barrier_semaphore()
    for who in (partner, mate_id, ext_id):
        pl.semaphore_signal(barrier, inc=1, device_id=who, device_id_type=pl.DeviceIdType.MESH)

    loads = []
    for c, piece in enumerate(pieces):
        pair = (
            pltpu.make_async_copy(text_hbm.at[piece], text_x.at[piece], load_sem.at[0, c]),
            pltpu.make_async_copy(image_hbm.at[piece], image_x.at[piece], load_sem.at[1, c]),
        )
        for copy in pair:
            copy.start()
        loads.append(pair)

    def remote(src, dst, kind, c, who):
        return pltpu.make_async_remote_copy(
            src_ref=src,
            dst_ref=dst,
            send_sem=send_sem.at[kind, c],
            recv_sem=recv_sem.at[kind, c],
            device_id=who,
            device_id_type=pl.DeviceIdType.MESH,
        )

    def send(*args):
        copy = remote(*args)
        copy.start()
        return copy

    ext_text, mate_text, partner_image = [], [], []
    for c, piece in enumerate(pieces):
        loads[c][0].wait()
        values = text_x[piece, :]
        inverse = inverse_norm(values)
        text_inv[piece, :] = inverse
        text_low[piece, :] = (values * inverse).astype(jnp.bfloat16)
        if c == 0:
            pl.semaphore_wait(barrier, 3)
        own = text_low.at[piece]
        ext_text.append(remote(own, text_low.at[pl.ds(2 * rows + c * step, step)], 0, c, ext_id))
        pl.when(leads)(ext_text[c].start)
        mate_text.append(send(own, text_low.at[pl.ds(rows + c * step, step)], 1, c, mate_id))
        loads[c][1].wait()
        values = image_x[piece, :]
        inverse = inverse_norm(values)
        image_inv[piece, :] = inverse
        image_low[piece, :] = (values * inverse).astype(jnp.bfloat16)
        own = image_low.at[piece]
        partner_image.append(remote(own, image_low.at[pl.ds(rows + c * step, step)], 2, c, partner))
        pl.when(leads)(partner_image[c].start)

    scale = scale_ref[0, 0]
    offset = offset_ref[0, 0]

    def fill(text_at, text_rows, image_at, image_rows, diagonal=False):
        texts = pl.ds(text_at, text_rows)
        images = pl.ds(image_at, image_rows)
        scores = scale * dot(text_low[texts, :], image_low[images, :], NT) + offset
        if diagonal:
            row = lax.broadcasted_iota(jnp.int32, scores.shape, 0)
            col = lax.broadcasted_iota(jnp.int32, scores.shape, 1)
            label = jnp.where(row == col, jnp.float32(1.0), jnp.float32(-1.0))
            values = -label * scale * (1.0 / (1.0 + jnp.exp(label * scores)))
        else:
            values = scale * (1.0 / (1.0 + jnp.exp(-scores)))
        coef[texts, images] = values.astype(jnp.bfloat16)

    def terms(texts):
        return jnp.dot(coef[texts, :], image_low[...], preferred_element_type=jnp.float32)

    fill(0, rows, 0, rows, diagonal=True)

    @pl.when(hands_over)
    def _():
        for c in range(EARLY):
            ext_text[c].wait_send()
            partner_image[c].wait_send()
        pl.semaphore_signal(
            turn, inc=1, device_id=mate_id, device_id_type=pl.DeviceIdType.MESH
        )

    @pl.when(jnp.logical_not(leads))
    def _():
        pl.semaphore_wait(turn, 1)
        for c in range(PIECES):
            ext_text[c].start()
            partner_image[c].start()

    for copy in mate_text:
        copy.wait_recv()
    fill(rows, rows, 0, rows)
    for copy in partner_image:
        copy.wait_recv()
    fill(0, 2 * rows, rows, rows)
    for copy in ext_text:
        copy.wait_recv()
    fill(2 * rows, rows, 0, 2 * rows)
    partner_coef[...] = coef[:, rows:].T

    ext_send[...] = terms(pl.ds(2 * rows, rows)).astype(jnp.bfloat16)
    ext_terms = [
        send(ext_send.at[piece], ext_recv.at[piece], 3, c, ext_id)
        for c, piece in enumerate(pieces)
    ]
    image_send[...] = jnp.dot(
        partner_coef[...], text_low[...], preferred_element_type=jnp.float32
    ).astype(jnp.bfloat16)
    image_terms = [
        send(image_send.at[piece], image_recv.at[piece], 5, c, partner)
        for c, piece in enumerate(pieces)
    ]
    near_terms = terms(pl.ds(0, 2 * rows))
    mate_send[...] = near_terms[rows:].astype(jnp.bfloat16)
    mate_terms = [
        send(mate_send.at[piece], mate_recv.at[piece], 4, c, mate_id)
        for c, piece in enumerate(pieces)
    ]
    text_part[...] = near_terms[:rows]
    image_part[...] = dot(coef[:, :rows], text_low[...], TN)

    for c, piece in enumerate(pieces):
        mate_terms[c].wait_recv()
        ext_terms[c].wait_recv()
        direction = (
            text_part[piece, :]
            + mate_recv[piece, :].astype(jnp.float32)
            + ext_recv[piece, :].astype(jnp.float32)
        )
        text_out[piece, :] = backward_norm(text_x[piece, :], text_inv[piece, :], direction)
        image_terms[c].wait_recv()
        direction = image_part[piece, :] + image_recv[piece, :].astype(jnp.float32)
        image_out[piece, :] = backward_norm(image_x[piece, :], image_inv[piece, :], direction)

    @pl.when(jnp.logical_not(hands_over))
    def _():
        for c in range(EARLY):
            ext_text[c].wait_send()
            partner_image[c].wait_send()

    for copies in (
        ext_text[EARLY:], partner_image[EARLY:], mate_text, ext_terms, mate_terms, image_terms
    ):
        for copy in copies:
            copy.wait_send()


def store(image_ref, text_ref, image_out, text_out, sem):
    step = image_ref.shape[0] // PIECES
    copies = []
    for c in range(PIECES):
        piece = pl.ds(c * step, step)
        copies += [
            pltpu.make_async_copy(image_ref.at[piece], image_out.at[piece], sem.at[0, c]),
            pltpu.make_async_copy(text_ref.at[piece], text_out.at[piece], sem.at[1, c]),
        ]
    for copy in copies:
        copy.start()
    for copy in copies:
        copy.wait()


def shards(groups, image, text, scale, offset):
    rows, width = image.shape
    full = pltpu.VMEM
    f32, low = jnp.float32, jnp.bfloat16
    image = pltpu.with_memory_space_constraint(image, pltpu.HBM)
    text = pltpu.with_memory_space_constraint(text, pltpu.HBM)
    grads = pl.pallas_call(
        functools.partial(kernel, groups, rows),
        out_shape=(jax.ShapeDtypeStruct((rows, width), f32),) * 2,
        in_specs=[pl.BlockSpec(memory_space=pltpu.SMEM)] * 2
        + [pl.BlockSpec(memory_space=pltpu.HBM)] * 2,
        out_specs=(pl.BlockSpec(memory_space=pltpu.VMEM),) * 2,
        scratch_shapes=[
            full((rows, width), f32),
            full((rows, width), f32),
            full((rows, 1), f32),
            full((rows, 1), f32),
            full((2 * rows, width), low),
            full((3 * rows, width), low),
            full((3 * rows, 2 * rows), low),
            full((rows, 3 * rows), low),
            full((rows, width), f32),
            full((rows, width), f32),
        ]
        + [full((rows, width), low)] * 6
        + [
            pltpu.SemaphoreType.DMA((2, PIECES)),
            pltpu.SemaphoreType.DMA((6, PIECES)),
            pltpu.SemaphoreType.DMA((6, PIECES)),
            pltpu.SemaphoreType.REGULAR,
        ],
        compiler_params=pltpu.CompilerParams(
            collective_id=0, has_side_effects=True, vmem_limit_bytes=32 * 1024 * 1024
        ),
        cost_estimate=pl.CostEstimate(
            flops=36 * rows * rows * width,
            bytes_accessed=16 * rows * width,
            transcendentals=6 * rows * rows,
        ),
    )(scale.reshape(1, 1), offset.reshape(1, 1), image, text)
    return tuple(
        pl.pallas_call(
            store,
            out_shape=(jax.ShapeDtypeStruct((rows, width), f32),) * 2,
            in_specs=[pl.BlockSpec(memory_space=pl.ANY)] * 2,
            out_specs=(pl.BlockSpec(memory_space=pltpu.HBM),) * 2,
            scratch_shapes=[pltpu.SemaphoreType.DMA((2, PIECES))],
            compiler_params=pltpu.CompilerParams(vmem_limit_bytes=16 * 1024 * 1024),
        )(*grads)
    )


def solution(mesh):
    if mesh.shape["sub"] != 2 or mesh.shape["dp"] % 4 or mesh.shape["dp"] < 4:
        raise ValueError("unsupported mesh")
    placed = (P(("dp", "sub"), None), P(("dp", "sub"), None), P(), P())
    return jax.shard_map(
        functools.partial(shards, mesh.shape["dp"]),
        mesh=mesh,
        in_specs=placed,
        out_specs=(P(("dp", "sub"), None), P(("dp", "sub"), None)),
        check_vma=False,
    )
```

```python
import functools

import jax
import jax.numpy as jnp
from jax import lax
from jax.experimental import pallas as pl
from jax.experimental.pallas import tpu as pltpu
from jax.sharding import PartitionSpec as P

PIECES = 4
EARLY = 1
NT = (((1,), (1,)), ((), ()))
TN = (((0,), (0,)), ((), ()))


def dot(a, b, dims):
    return lax.dot_general(a, b, dims, preferred_element_type=jnp.float32)


def inverse_norm(values):
    return lax.rsqrt(jnp.sum(values * values, axis=-1, keepdims=True) + 1e-06)


def backward_norm(values, inverse, direction):
    unit = values * inverse
    return (direction - unit * jnp.sum(unit * direction, axis=-1, keepdims=True)) * inverse


def kernel(
    groups, rows,
    scale_ref, offset_ref, image_hbm, text_hbm,
    image_out, text_out,
    image_x, text_x, image_inv, text_inv,
    image_low, text_low, coef, partner_coef,
    image_part, text_part,
    image_send, mate_send, ext_send,
    image_recv, mate_recv, ext_recv,
    load_sem, send_sem, recv_sem, turn,
):
    g = lax.axis_index("dp")
    s = lax.axis_index("sub")
    odd = lax.rem(g, 2)
    mate = g + 1 - 2 * odd
    ext = lax.rem(g - 1 + 2 * odd + groups, groups)
    partner = (g, 1 - s)
    mate_id = (mate, s)
    ext_id = (ext, s)

    leads = lax.rem((g + 1) // 2, 2) == 1

    step = rows // PIECES
    pieces = [pl.ds(c * step, step) for c in range(PIECES)]

    barrier = pltpu.get_barrier_semaphore()
    for who in (partner, mate_id, ext_id):
        pl.semaphore_signal(barrier, inc=1, device_id=who, device_id_type=pl.DeviceIdType.MESH)

    loads = []
    for c, piece in enumerate(pieces):
        pair = (
            pltpu.make_async_copy(text_hbm.at[piece], text_x.at[piece], load_sem.at[0, c]),
            pltpu.make_async_copy(image_hbm.at[piece], image_x.at[piece], load_sem.at[1, c]),
        )
        for copy in pair:
            copy.start()
        loads.append(pair)

    def remote(src, dst, kind, c, who):
        return pltpu.make_async_remote_copy(
            src_ref=src,
            dst_ref=dst,
            send_sem=send_sem.at[kind, c],
            recv_sem=recv_sem.at[kind, c],
            device_id=who,
            device_id_type=pl.DeviceIdType.MESH,
        )

    def send(*args):
        copy = remote(*args)
        copy.start()
        return copy

    ext_text, mate_text, partner_image = [], [], []
    for c, piece in enumerate(pieces):
        loads[c][0].wait()
        values = text_x[piece, :]
        inverse = inverse_norm(values)
        text_inv[piece, :] = inverse
        text_low[piece, :] = (values * inverse).astype(jnp.bfloat16)
        if c == 0:
            pl.semaphore_wait(barrier, 3)
        own = text_low.at[piece]
        ext_text.append(remote(own, text_low.at[pl.ds(2 * rows + c * step, step)], 0, c, ext_id))
        pl.when(leads)(ext_text[c].start)
        mate_text.append(send(own, text_low.at[pl.ds(rows + c * step, step)], 1, c, mate_id))
        loads[c][1].wait()
        values = image_x[piece, :]
        inverse = inverse_norm(values)
        image_inv[piece, :] = inverse
        image_low[piece, :] = (values * inverse).astype(jnp.bfloat16)
        own = image_low.at[piece]
        partner_image.append(remote(own, image_low.at[pl.ds(rows + c * step, step)], 2, c, partner))
        pl.when(leads)(partner_image[c].start)

    scale = scale_ref[0, 0]
    offset = offset_ref[0, 0]

    def fill(text_at, text_rows, image_at, image_rows, diagonal=False):
        texts = pl.ds(text_at, text_rows)
        images = pl.ds(image_at, image_rows)
        scores = scale * dot(text_low[texts, :], image_low[images, :], NT) + offset
        if diagonal:
            row = lax.broadcasted_iota(jnp.int32, scores.shape, 0)
            col = lax.broadcasted_iota(jnp.int32, scores.shape, 1)
            label = jnp.where(row == col, jnp.float32(1.0), jnp.float32(-1.0))
            values = -label * scale * (1.0 / (1.0 + jnp.exp(label * scores)))
        else:
            values = scale * (1.0 / (1.0 + jnp.exp(-scores)))
        coef[texts, images] = values.astype(jnp.bfloat16)

    def terms(texts):
        return jnp.dot(coef[texts, :], image_low[...], preferred_element_type=jnp.float32)

    fill(0, rows, 0, rows, diagonal=True)

    @pl.when(leads)
    def _():
        for c in range(EARLY):
            ext_text[c].wait_send()
            partner_image[c].wait_send()
        pl.semaphore_signal(
            turn, inc=1, device_id=mate_id, device_id_type=pl.DeviceIdType.MESH
        )

    @pl.when(jnp.logical_not(leads))
    def _():
        pl.semaphore_wait(turn, 1)
        for c in range(PIECES):
            ext_text[c].start()
            partner_image[c].start()

    for copy in mate_text:
        copy.wait_recv()
    fill(rows, rows, 0, rows)
    for copy in partner_image:
        copy.wait_recv()
    fill(0, 2 * rows, rows, rows)
    for copy in ext_text:
        copy.wait_recv()
    fill(2 * rows, rows, 0, 2 * rows)
    partner_coef[...] = coef[:, rows:].T

    ext_send[...] = terms(pl.ds(2 * rows, rows)).astype(jnp.bfloat16)
    ext_terms = [
        send(ext_send.at[piece], ext_recv.at[piece], 3, c, ext_id)
        for c, piece in enumerate(pieces)
    ]
    image_send[...] = jnp.dot(
        partner_coef[...], text_low[...], preferred_element_type=jnp.float32
    ).astype(jnp.bfloat16)
    image_terms = [
        send(image_send.at[piece], image_recv.at[piece], 5, c, partner)
        for c, piece in enumerate(pieces)
    ]
    near_terms = terms(pl.ds(0, 2 * rows))
    mate_send[...] = near_terms[rows:].astype(jnp.bfloat16)
    mate_terms = [
        send(mate_send.at[piece], mate_recv.at[piece], 4, c, mate_id)
        for c, piece in enumerate(pieces)
    ]
    text_part[...] = near_terms[:rows]
    image_part[...] = dot(coef[:, :rows], text_low[...], TN)

    for c, piece in enumerate(pieces):
        mate_terms[c].wait_recv()
        ext_terms[c].wait_recv()
        direction = (
            text_part[piece, :]
            + mate_recv[piece, :].astype(jnp.float32)
            + ext_recv[piece, :].astype(jnp.float32)
        )
        text_out[piece, :] = backward_norm(text_x[piece, :], text_inv[piece, :], direction)
        image_terms[c].wait_recv()
        direction = image_part[piece, :] + image_recv[piece, :].astype(jnp.float32)
        image_out[piece, :] = backward_norm(image_x[piece, :], image_inv[piece, :], direction)

    @pl.when(jnp.logical_not(leads))
    def _():
        for c in range(EARLY):
            ext_text[c].wait_send()
            partner_image[c].wait_send()

    for copies in (
        ext_text[EARLY:], partner_image[EARLY:], mate_text, ext_terms, mate_terms, image_terms
    ):
        for copy in copies:
            copy.wait_send()


def store(image_ref, text_ref, image_out, text_out, sem):
    step = image_ref.shape[0] // PIECES
    copies = []
    for c in range(PIECES):
        piece = pl.ds(c * step, step)
        copies += [
            pltpu.make_async_copy(image_ref.at[piece], image_out.at[piece], sem.at[0, c]),
            pltpu.make_async_copy(text_ref.at[piece], text_out.at[piece], sem.at[1, c]),
        ]
    for copy in copies:
        copy.start()
    for copy in copies:
        copy.wait()


def shards(groups, image, text, scale, offset):
    rows, width = image.shape
    full = pltpu.VMEM
    f32, low = jnp.float32, jnp.bfloat16
    image = pltpu.with_memory_space_constraint(image, pltpu.HBM)
    text = pltpu.with_memory_space_constraint(text, pltpu.HBM)
    grads = pl.pallas_call(
        functools.partial(kernel, groups, rows),
        out_shape=(jax.ShapeDtypeStruct((rows, width), f32),) * 2,
        in_specs=[pl.BlockSpec(memory_space=pltpu.SMEM)] * 2
        + [pl.BlockSpec(memory_space=pltpu.HBM)] * 2,
        out_specs=(pl.BlockSpec(memory_space=pltpu.VMEM),) * 2,
        scratch_shapes=[
            full((rows, width), f32),
            full((rows, width), f32),
            full((rows, 1), f32),
            full((rows, 1), f32),
            full((2 * rows, width), low),
            full((3 * rows, width), low),
            full((3 * rows, 2 * rows), low),
            full((rows, 3 * rows), low),
            full((rows, width), f32),
            full((rows, width), f32),
        ]
        + [full((rows, width), low)] * 6
        + [
            pltpu.SemaphoreType.DMA((2, PIECES)),
            pltpu.SemaphoreType.DMA((6, PIECES)),
            pltpu.SemaphoreType.DMA((6, PIECES)),
            pltpu.SemaphoreType.REGULAR,
        ],
        compiler_params=pltpu.CompilerParams(
            collective_id=0, has_side_effects=True, vmem_limit_bytes=32 * 1024 * 1024
        ),
        cost_estimate=pl.CostEstimate(
            flops=36 * rows * rows * width,
            bytes_accessed=16 * rows * width,
            transcendentals=6 * rows * rows,
        ),
    )(scale.reshape(1, 1), offset.reshape(1, 1), image, text)
    return tuple(
        pl.pallas_call(
            store,
            out_shape=(jax.ShapeDtypeStruct((rows, width), f32),) * 2,
            in_specs=[pl.BlockSpec(memory_space=pl.ANY)] * 2,
            out_specs=(pl.BlockSpec(memory_space=pltpu.HBM),) * 2,
            scratch_shapes=[pltpu.SemaphoreType.DMA((2, PIECES))],
            compiler_params=pltpu.CompilerParams(vmem_limit_bytes=16 * 1024 * 1024),
        )(*grads)
    )


def solution(mesh):
    if mesh.shape["sub"] != 2 or mesh.shape["dp"] % 4 or mesh.shape["dp"] < 4:
        raise ValueError("unsupported mesh")
    placed = (P(("dp", "sub"), None), P(("dp", "sub"), None), P(), P())
    return jax.shard_map(
        functools.partial(shards, mesh.shape["dp"]),
        mesh=mesh,
        in_specs=placed,
        out_specs=(P(("dp", "sub"), None), P(("dp", "sub"), None)),
        check_vma=False,
    )
```

```python
import functools

import jax
import jax.numpy as jnp
from jax import lax
from jax.experimental import pallas as pl
from jax.experimental.pallas import tpu as pltpu
from jax.sharding import PartitionSpec as P

PIECES = 4
EARLY = 3
NT = (((1,), (1,)), ((), ()))
TN = (((0,), (0,)), ((), ()))


def dot(a, b, dims):
    return lax.dot_general(a, b, dims, preferred_element_type=jnp.float32)


def inverse_norm(values):
    return lax.rsqrt(jnp.sum(values * values, axis=-1, keepdims=True) + 1e-06)


def backward_norm(values, inverse, direction):
    unit = values * inverse
    return (direction - unit * jnp.sum(unit * direction, axis=-1, keepdims=True)) * inverse


def kernel(
    groups, rows,
    scale_hbm, offset_hbm, image_hbm, text_hbm,
    image_out, text_out,
    image_x, text_x, image_inv, text_inv,
    image_low, text_low, coef, partner_coef,
    image_part, text_part,
    image_send, mate_send, ext_send,
    image_recv, mate_recv, ext_recv,
    scale_ref, offset_ref,
    load_sem, scalar_sem, send_sem, recv_sem, turn, later_turn,
):
    g = lax.axis_index("dp")
    s = lax.axis_index("sub")
    odd = lax.rem(g, 2)
    mate = g + 1 - 2 * odd
    ext = lax.rem(g - 1 + 2 * odd + groups, groups)
    partner = (g, 1 - s)
    mate_id = (mate, s)
    ext_id = (ext, s)

    wrap = jnp.logical_or(g == 0, g == groups - 1)
    near = jnp.logical_and(lax.rem((g + 1) // 2, 2) == 1, g != groups - 2)
    leads = jnp.logical_or(near, wrap)
    hands_over = jnp.logical_and(leads, g > 1)

    step = rows // PIECES
    pieces = [pl.ds(c * step, step) for c in range(PIECES)]

    barrier = pltpu.get_barrier_semaphore()
    for who in (partner, mate_id, ext_id):
        pl.semaphore_signal(barrier, inc=1, device_id=who, device_id_type=pl.DeviceIdType.MESH)

    scalars = [
        pltpu.make_async_copy(scale_hbm, scale_ref, scalar_sem.at[0]),
        pltpu.make_async_copy(offset_hbm, offset_ref, scalar_sem.at[1]),
    ]
    loads = []
    for c, piece in enumerate(pieces):
        pair = (
            pltpu.make_async_copy(text_hbm.at[piece], text_x.at[piece], load_sem.at[0, c]),
            pltpu.make_async_copy(image_hbm.at[piece], image_x.at[piece], load_sem.at[1, c]),
        )
        for copy in pair:
            copy.start()
        loads.append(pair)

    for copy in scalars:
        copy.start()

    def remote(src, dst, kind, c, who):
        return pltpu.make_async_remote_copy(
            src_ref=src,
            dst_ref=dst,
            send_sem=send_sem.at[kind, c],
            recv_sem=recv_sem.at[kind, c],
            device_id=who,
            device_id_type=pl.DeviceIdType.MESH,
        )

    def send(*args):
        copy = remote(*args)
        copy.start()
        return copy

    ext_text, mate_text, partner_image = [], [], []
    for c, piece in enumerate(pieces):
        loads[c][0].wait()
        values = text_x[piece, :]
        inverse = inverse_norm(values)
        text_inv[piece, :] = inverse
        text_low[piece, :] = (values * inverse).astype(jnp.bfloat16)
        if c == 0:
            pl.semaphore_wait(barrier, 3)
        own = text_low.at[piece]
        ext_text.append(remote(own, text_low.at[pl.ds(2 * rows + c * step, step)], 0, c, ext_id))
        pl.when(leads)(ext_text[c].start)
        mate_text.append(send(own, text_low.at[pl.ds(rows + c * step, step)], 1, c, mate_id))
        loads[c][1].wait()
        values = image_x[piece, :]
        inverse = inverse_norm(values)
        image_inv[piece, :] = inverse
        image_low[piece, :] = (values * inverse).astype(jnp.bfloat16)
        own = image_low.at[piece]
        partner_image.append(remote(own, image_low.at[pl.ds(rows + c * step, step)], 2, c, partner))
        pl.when(leads)(partner_image[c].start)

    for copy in scalars:
        copy.wait()
    scale = scale_ref[0, 0]
    offset = offset_ref[0, 0]

    def fill(text_at, text_rows, image_at, image_rows, diagonal=False):
        texts = pl.ds(text_at, text_rows)
        images = pl.ds(image_at, image_rows)
        scores = scale * dot(text_low[texts, :], image_low[images, :], NT) + offset
        if diagonal:
            row = lax.broadcasted_iota(jnp.int32, scores.shape, 0)
            col = lax.broadcasted_iota(jnp.int32, scores.shape, 1)
            label = jnp.where(row == col, jnp.float32(1.0), jnp.float32(-1.0))
            values = -label * scale * (1.0 / (1.0 + jnp.exp(label * scores)))
        else:
            values = scale * (1.0 / (1.0 + jnp.exp(-scores)))
        coef[texts, images] = values.astype(jnp.bfloat16)

    def terms(texts):
        return jnp.dot(coef[texts, :], image_low[...], preferred_element_type=jnp.float32)

    fill(0, rows, 0, rows, diagonal=True)

    @pl.when(hands_over)
    def _():
        for c in range(EARLY):
            ext_text[c].wait_send()
            partner_image[c].wait_send()
        pl.semaphore_signal(
            turn, inc=1, device_id=mate_id, device_id_type=pl.DeviceIdType.MESH
        )

    @pl.when(jnp.logical_not(leads))
    def _():
        pl.semaphore_wait(turn, 1)
        for c in range(PIECES):
            ext_text[c].start()
            partner_image[c].start()

    for copy in mate_text:
        copy.wait_recv()
    fill(rows, rows, 0, rows)
    for copy in partner_image:
        copy.wait_recv()
    fill(0, 2 * rows, rows, rows)
    for copy in ext_text:
        copy.wait_recv()
    fill(2 * rows, rows, 0, 2 * rows)
    partner_coef[...] = coef[:, rows:].T

    ext_send[...] = terms(pl.ds(2 * rows, rows)).astype(jnp.bfloat16)
    ext_terms = [
        remote(ext_send.at[piece], ext_recv.at[piece], 3, c, ext_id)
        for c, piece in enumerate(pieces)
    ]

    @pl.when(g != groups - 2)
    def _():
        for copy in ext_terms:
            copy.start()

    image_send[...] = jnp.dot(
        partner_coef[...], text_low[...], preferred_element_type=jnp.float32
    ).astype(jnp.bfloat16)
    image_terms = [
        send(image_send.at[piece], image_recv.at[piece], 5, c, partner)
        for c, piece in enumerate(pieces)
    ]
    near_terms = terms(pl.ds(0, 2 * rows))
    mate_send[...] = near_terms[rows:].astype(jnp.bfloat16)
    mate_terms = [
        send(mate_send.at[piece], mate_recv.at[piece], 4, c, mate_id)
        for c, piece in enumerate(pieces)
    ]
    text_part[...] = near_terms[:rows]
    image_part[...] = dot(coef[:, :rows], text_low[...], TN)

    @pl.when(g == groups - 1)
    def _():
        for copy in ext_terms[:EARLY]:
            copy.wait_send()
        pl.semaphore_signal(
            later_turn, inc=1, device_id=mate_id, device_id_type=pl.DeviceIdType.MESH
        )

    @pl.when(g == groups - 2)
    def _():
        pl.semaphore_wait(later_turn, 1)
        for copy in ext_terms:
            copy.start()

    for c, piece in enumerate(pieces):
        mate_terms[c].wait_recv()
        ext_terms[c].wait_recv()
        direction = (
            text_part[piece, :]
            + mate_recv[piece, :].astype(jnp.float32)
            + ext_recv[piece, :].astype(jnp.float32)
        )
        text_out[piece, :] = backward_norm(text_x[piece, :], text_inv[piece, :], direction)
        image_terms[c].wait_recv()
        direction = image_part[piece, :] + image_recv[piece, :].astype(jnp.float32)
        image_out[piece, :] = backward_norm(image_x[piece, :], image_inv[piece, :], direction)

    @pl.when(jnp.logical_not(hands_over))
    def _():
        for c in range(EARLY):
            ext_text[c].wait_send()
            partner_image[c].wait_send()

    @pl.when(g != groups - 1)
    def _():
        for copy in ext_terms[:EARLY]:
            copy.wait_send()

    for copies in (
        ext_text[EARLY:], partner_image[EARLY:], mate_text,
        ext_terms[EARLY:], mate_terms, image_terms,
    ):
        for copy in copies:
            copy.wait_send()


def store(image_ref, text_ref, image_out, text_out, sem):
    step = image_ref.shape[0] // PIECES
    copies = []
    for c in range(PIECES):
        piece = pl.ds(c * step, step)
        copies += [
            pltpu.make_async_copy(image_ref.at[piece], image_out.at[piece], sem.at[0, c]),
            pltpu.make_async_copy(text_ref.at[piece], text_out.at[piece], sem.at[1, c]),
        ]
    for copy in copies:
        copy.start()
    for copy in copies:
        copy.wait()


def shards(groups, image, text, scale, offset):
    rows, width = image.shape
    full = pltpu.VMEM
    f32, low = jnp.float32, jnp.bfloat16
    scale = scale.reshape(1, 1)
    offset = offset.reshape(1, 1)
    image = pltpu.with_memory_space_constraint(image, pltpu.HBM)
    text = pltpu.with_memory_space_constraint(text, pltpu.HBM)
    grads = pl.pallas_call(
        functools.partial(kernel, groups, rows),
        out_shape=(jax.ShapeDtypeStruct((rows, width), f32),) * 2,
        in_specs=[pl.BlockSpec(memory_space=pltpu.HBM)] * 4,
        out_specs=(pl.BlockSpec(memory_space=pltpu.VMEM),) * 2,
        scratch_shapes=[
            full((rows, width), f32),
            full((rows, width), f32),
            full((rows, 1), f32),
            full((rows, 1), f32),
            full((2 * rows, width), low),
            full((3 * rows, width), low),
            full((3 * rows, 2 * rows), low),
            full((rows, 3 * rows), low),
            full((rows, width), f32),
            full((rows, width), f32),
        ]
        + [full((rows, width), low)] * 6
        + [
            pltpu.SMEM((1, 1), f32),
            pltpu.SMEM((1, 1), f32),
            pltpu.SemaphoreType.DMA((2, PIECES)),
            pltpu.SemaphoreType.DMA((2,)),
            pltpu.SemaphoreType.DMA((6, PIECES)),
            pltpu.SemaphoreType.DMA((6, PIECES)),
            pltpu.SemaphoreType.REGULAR,
            pltpu.SemaphoreType.REGULAR,
        ],
        compiler_params=pltpu.CompilerParams(
            collective_id=0, has_side_effects=True, vmem_limit_bytes=32 * 1024 * 1024
        ),
        cost_estimate=pl.CostEstimate(
            flops=36 * rows * rows * width,
            bytes_accessed=16 * rows * width,
            transcendentals=6 * rows * rows,
        ),
    )(scale, offset, image, text)
    return tuple(
        pl.pallas_call(
            store,
            out_shape=(jax.ShapeDtypeStruct((rows, width), f32),) * 2,
            in_specs=[pl.BlockSpec(memory_space=pl.ANY)] * 2,
            out_specs=(pl.BlockSpec(memory_space=pltpu.HBM),) * 2,
            scratch_shapes=[pltpu.SemaphoreType.DMA((2, PIECES))],
            compiler_params=pltpu.CompilerParams(vmem_limit_bytes=16 * 1024 * 1024),
        )(*grads)
    )


def solution(mesh):
    if mesh.shape["sub"] != 2 or mesh.shape["dp"] % 4 or mesh.shape["dp"] < 4:
        raise ValueError("unsupported mesh")
    placed = (P(("dp", "sub"), None), P(("dp", "sub"), None), P(), P())
    return jax.shard_map(
        functools.partial(shards, mesh.shape["dp"]),
        mesh=mesh,
        in_specs=placed,
        out_specs=(P(("dp", "sub"), None), P(("dp", "sub"), None)),
        check_vma=False,
    )
```

```python
import functools

import jax
import jax.numpy as jnp
from jax import lax
from jax.experimental import pallas as pl
from jax.experimental.pallas import tpu as pltpu
from jax.sharding import PartitionSpec as P

PIECES = 4
EARLY = 2
NT = (((1,), (1,)), ((), ()))
TN = (((0,), (0,)), ((), ()))


def dot(a, b, dims):
    return lax.dot_general(a, b, dims, preferred_element_type=jnp.float32)


def inverse_norm(values):
    return lax.rsqrt(jnp.sum(values * values, axis=-1, keepdims=True) + 1e-06)


def backward_norm(values, inverse, direction):
    unit = values * inverse
    return (direction - unit * jnp.sum(unit * direction, axis=-1, keepdims=True)) * inverse


def kernel(
    groups, rows,
    scale_ref, offset_ref, image_hbm, text_hbm,
    image_out, text_out,
    image_x, text_x, image_inv, text_inv,
    image_low, text_low, coef, partner_coef,
    image_part, text_part,
    image_send, mate_send, ext_send,
    image_recv, mate_recv, ext_recv,
    load_sem, send_sem, recv_sem, turn,
):
    g = lax.axis_index("dp")
    s = lax.axis_index("sub")
    odd = lax.rem(g, 2)
    mate = g + 1 - 2 * odd
    ext = lax.rem(g - 1 + 2 * odd + groups, groups)
    partner = (g, 1 - s)
    mate_id = (mate, s)
    ext_id = (ext, s)

    leads = jnp.logical_or(lax.rem((g + 1) // 2, 2) == 0, g == 1)
    hands_over = jnp.logical_and(leads, g > 1)

    step = rows // PIECES
    pieces = [pl.ds(c * step, step) for c in range(PIECES)]

    barrier = pltpu.get_barrier_semaphore()
    for who in (partner, mate_id, ext_id):
        pl.semaphore_signal(barrier, inc=1, device_id=who, device_id_type=pl.DeviceIdType.MESH)

    loads = []
    for c, piece in enumerate(pieces):
        pair = (
            pltpu.make_async_copy(text_hbm.at[piece], text_x.at[piece], load_sem.at[0, c]),
            pltpu.make_async_copy(image_hbm.at[piece], image_x.at[piece], load_sem.at[1, c]),
        )
        for copy in pair:
            copy.start()
        loads.append(pair)

    def remote(src, dst, kind, c, who):
        return pltpu.make_async_remote_copy(
            src_ref=src,
            dst_ref=dst,
            send_sem=send_sem.at[kind, c],
            recv_sem=recv_sem.at[kind, c],
            device_id=who,
            device_id_type=pl.DeviceIdType.MESH,
        )

    def send(*args):
        copy = remote(*args)
        copy.start()
        return copy

    ext_text, mate_text, partner_image = [], [], []
    for c, piece in enumerate(pieces):
        loads[c][0].wait()
        values = text_x[piece, :]
        inverse = inverse_norm(values)
        text_inv[piece, :] = inverse
        text_low[piece, :] = (values * inverse).astype(jnp.bfloat16)
        if c == 0:
            pl.semaphore_wait(barrier, 3)
        own = text_low.at[piece]
        ext_text.append(remote(own, text_low.at[pl.ds(2 * rows + c * step, step)], 0, c, ext_id))
        pl.when(leads)(ext_text[c].start)
        mate_text.append(send(own, text_low.at[pl.ds(rows + c * step, step)], 1, c, mate_id))
        loads[c][1].wait()
        values = image_x[piece, :]
        inverse = inverse_norm(values)
        image_inv[piece, :] = inverse
        image_low[piece, :] = (values * inverse).astype(jnp.bfloat16)
        own = image_low.at[piece]
        partner_image.append(remote(own, image_low.at[pl.ds(rows + c * step, step)], 2, c, partner))
        pl.when(leads)(partner_image[c].start)

    scale = scale_ref[0, 0]
    offset = offset_ref[0, 0]

    def fill(text_at, text_rows, image_at, image_rows, diagonal=False):
        texts = pl.ds(text_at, text_rows)
        images = pl.ds(image_at, image_rows)
        scores = scale * dot(text_low[texts, :], image_low[images, :], NT) + offset
        if diagonal:
            row = lax.broadcasted_iota(jnp.int32, scores.shape, 0)
            col = lax.broadcasted_iota(jnp.int32, scores.shape, 1)
            label = jnp.where(row == col, jnp.float32(1.0), jnp.float32(-1.0))
            values = -label * scale * (1.0 / (1.0 + jnp.exp(label * scores)))
        else:
            values = scale * (1.0 / (1.0 + jnp.exp(-scores)))
        coef[texts, images] = values.astype(jnp.bfloat16)

    def terms(texts):
        return jnp.dot(coef[texts, :], image_low[...], preferred_element_type=jnp.float32)

    fill(0, rows, 0, rows, diagonal=True)

    @pl.when(hands_over)
    def _():
        for c in range(EARLY):
            ext_text[c].wait_send()
            partner_image[c].wait_send()
        pl.semaphore_signal(
            turn, inc=1, device_id=mate_id, device_id_type=pl.DeviceIdType.MESH
        )

    @pl.when(jnp.logical_not(leads))
    def _():
        pl.semaphore_wait(turn, 1)
        for c in range(PIECES):
            ext_text[c].start()
            partner_image[c].start()

    for copy in mate_text:
        copy.wait_recv()
    fill(rows, rows, 0, rows)
    for copy in partner_image:
        copy.wait_recv()
    fill(0, 2 * rows, rows, rows)
    for copy in ext_text:
        copy.wait_recv()
    fill(2 * rows, rows, 0, 2 * rows)
    partner_coef[...] = coef[:, rows:].T

    ext_send[...] = terms(pl.ds(2 * rows, rows)).astype(jnp.bfloat16)
    ext_terms = [
        send(ext_send.at[piece], ext_recv.at[piece], 3, c, ext_id)
        for c, piece in enumerate(pieces)
    ]
    image_send[...] = jnp.dot(
        partner_coef[...], text_low[...], preferred_element_type=jnp.float32
    ).astype(jnp.bfloat16)
    image_terms = [
        send(image_send.at[piece], image_recv.at[piece], 5, c, partner)
        for c, piece in enumerate(pieces)
    ]
    near_terms = terms(pl.ds(0, 2 * rows))
    mate_send[...] = near_terms[rows:].astype(jnp.bfloat16)
    mate_terms = [
        send(mate_send.at[piece], mate_recv.at[piece], 4, c, mate_id)
        for c, piece in enumerate(pieces)
    ]
    text_part[...] = near_terms[:rows]
    image_part[...] = dot(coef[:, :rows], text_low[...], TN)

    for c, piece in enumerate(pieces):
        mate_terms[c].wait_recv()
        ext_terms[c].wait_recv()
        direction = (
            text_part[piece, :]
            + mate_recv[piece, :].astype(jnp.float32)
            + ext_recv[piece, :].astype(jnp.float32)
        )
        text_out[piece, :] = backward_norm(text_x[piece, :], text_inv[piece, :], direction)
        image_terms[c].wait_recv()
        direction = image_part[piece, :] + image_recv[piece, :].astype(jnp.float32)
        image_out[piece, :] = backward_norm(image_x[piece, :], image_inv[piece, :], direction)

    @pl.when(jnp.logical_not(hands_over))
    def _():
        for c in range(EARLY):
            ext_text[c].wait_send()
            partner_image[c].wait_send()

    for copies in (
        ext_text[EARLY:], partner_image[EARLY:], mate_text, ext_terms, mate_terms, image_terms
    ):
        for copy in copies:
            copy.wait_send()


def store(image_ref, text_ref, image_out, text_out, sem):
    step = image_ref.shape[0] // PIECES
    copies = []
    for c in range(PIECES):
        piece = pl.ds(c * step, step)
        copies += [
            pltpu.make_async_copy(image_ref.at[piece], image_out.at[piece], sem.at[0, c]),
            pltpu.make_async_copy(text_ref.at[piece], text_out.at[piece], sem.at[1, c]),
        ]
    for copy in copies:
        copy.start()
    for copy in copies:
        copy.wait()


def shards(groups, image, text, scale, offset):
    rows, width = image.shape
    full = pltpu.VMEM
    f32, low = jnp.float32, jnp.bfloat16
    image = pltpu.with_memory_space_constraint(image, pltpu.HBM)
    text = pltpu.with_memory_space_constraint(text, pltpu.HBM)
    grads = pl.pallas_call(
        functools.partial(kernel, groups, rows),
        out_shape=(jax.ShapeDtypeStruct((rows, width), f32),) * 2,
        in_specs=[pl.BlockSpec(memory_space=pltpu.SMEM)] * 2
        + [pl.BlockSpec(memory_space=pltpu.HBM)] * 2,
        out_specs=(pl.BlockSpec(memory_space=pltpu.VMEM),) * 2,
        scratch_shapes=[
            full((rows, width), f32),
            full((rows, width), f32),
            full((rows, 1), f32),
            full((rows, 1), f32),
            full((2 * rows, width), low),
            full((3 * rows, width), low),
            full((3 * rows, 2 * rows), low),
            full((rows, 3 * rows), low),
            full((rows, width), f32),
            full((rows, width), f32),
        ]
        + [full((rows, width), low)] * 6
        + [
            pltpu.SemaphoreType.DMA((2, PIECES)),
            pltpu.SemaphoreType.DMA((6, PIECES)),
            pltpu.SemaphoreType.DMA((6, PIECES)),
            pltpu.SemaphoreType.REGULAR,
        ],
        compiler_params=pltpu.CompilerParams(
            collective_id=0, has_side_effects=True, vmem_limit_bytes=32 * 1024 * 1024
        ),
        cost_estimate=pl.CostEstimate(
            flops=36 * rows * rows * width,
            bytes_accessed=16 * rows * width,
            transcendentals=6 * rows * rows,
        ),
    )(scale.reshape(1, 1), offset.reshape(1, 1), image, text)
    return tuple(
        pl.pallas_call(
            store,
            out_shape=(jax.ShapeDtypeStruct((rows, width), f32),) * 2,
            in_specs=[pl.BlockSpec(memory_space=pl.ANY)] * 2,
            out_specs=(pl.BlockSpec(memory_space=pltpu.HBM),) * 2,
            scratch_shapes=[pltpu.SemaphoreType.DMA((2, PIECES))],
            compiler_params=pltpu.CompilerParams(vmem_limit_bytes=16 * 1024 * 1024),
        )(*grads)
    )


def solution(mesh):
    if mesh.shape["sub"] != 2 or mesh.shape["dp"] % 4 or mesh.shape["dp"] < 4:
        raise ValueError("unsupported mesh")
    placed = (P(("dp", "sub"), None), P(("dp", "sub"), None), P(), P())
    return jax.shard_map(
        functools.partial(shards, mesh.shape["dp"]),
        mesh=mesh,
        in_specs=placed,
        out_specs=(P(("dp", "sub"), None), P(("dp", "sub"), None)),
        check_vma=False,
    )
```

```python
import functools

import jax
import jax.numpy as jnp
from jax import lax
from jax.experimental import pallas as pl
from jax.experimental.pallas import tpu as pltpu
from jax.sharding import PartitionSpec as P

PIECES = 4
EARLY = 2
NT = (((1,), (1,)), ((), ()))
TN = (((0,), (0,)), ((), ()))


def dot(a, b, dims):
    return lax.dot_general(a, b, dims, preferred_element_type=jnp.float32)


def inverse_norm(values):
    return lax.rsqrt(jnp.sum(values * values, axis=-1, keepdims=True) + 1e-06)


def backward_norm(values, inverse, direction):
    unit = values * inverse
    return (direction - unit * jnp.sum(unit * direction, axis=-1, keepdims=True)) * inverse


def kernel(
    groups, rows,
    scale_ref, offset_ref, image_hbm, text_hbm,
    image_out, text_out,
    image_x, text_x, image_inv, text_inv,
    image_low, text_low, coef, partner_coef,
    image_part, text_part,
    image_send, mate_send, ext_send,
    image_recv, mate_recv, ext_recv,
    load_sem, send_sem, recv_sem, turn,
):
    g = lax.axis_index("dp")
    s = lax.axis_index("sub")
    odd = lax.rem(g, 2)
    mate = g + 1 - 2 * odd
    ext = lax.rem(g - 1 + 2 * odd + groups, groups)
    partner = (g, 1 - s)
    mate_id = (mate, s)
    ext_id = (ext, s)

    leads = jnp.logical_or(lax.rem((g + 1) // 2, 2) == 0, g < 3)
    hands_over = jnp.logical_and(leads, g > 3)

    step = rows // PIECES
    pieces = [pl.ds(c * step, step) for c in range(PIECES)]

    barrier = pltpu.get_barrier_semaphore()
    for who in (partner, mate_id, ext_id):
        pl.semaphore_signal(barrier, inc=1, device_id=who, device_id_type=pl.DeviceIdType.MESH)

    loads = []
    for c, piece in enumerate(pieces):
        pair = (
            pltpu.make_async_copy(text_hbm.at[piece], text_x.at[piece], load_sem.at[0, c]),
            pltpu.make_async_copy(image_hbm.at[piece], image_x.at[piece], load_sem.at[1, c]),
        )
        for copy in pair:
            copy.start()
        loads.append(pair)

    def remote(src, dst, kind, c, who):
        return pltpu.make_async_remote_copy(
            src_ref=src,
            dst_ref=dst,
            send_sem=send_sem.at[kind, c],
            recv_sem=recv_sem.at[kind, c],
            device_id=who,
            device_id_type=pl.DeviceIdType.MESH,
        )

    def send(*args):
        copy = remote(*args)
        copy.start()
        return copy

    ext_text, mate_text, partner_image = [], [], []
    for c, piece in enumerate(pieces):
        loads[c][0].wait()
        values = text_x[piece, :]
        inverse = inverse_norm(values)
        text_inv[piece, :] = inverse
        text_low[piece, :] = (values * inverse).astype(jnp.bfloat16)
        if c == 0:
            pl.semaphore_wait(barrier, 3)
        own = text_low.at[piece]
        ext_text.append(remote(own, text_low.at[pl.ds(2 * rows + c * step, step)], 0, c, ext_id))
        pl.when(leads)(ext_text[c].start)
        mate_text.append(send(own, text_low.at[pl.ds(rows + c * step, step)], 1, c, mate_id))
        loads[c][1].wait()
        values = image_x[piece, :]
        inverse = inverse_norm(values)
        image_inv[piece, :] = inverse
        image_low[piece, :] = (values * inverse).astype(jnp.bfloat16)
        own = image_low.at[piece]
        partner_image.append(remote(own, image_low.at[pl.ds(rows + c * step, step)], 2, c, partner))
        pl.when(leads)(partner_image[c].start)

    scale = scale_ref[0, 0]
    offset = offset_ref[0, 0]

    def fill(text_at, text_rows, image_at, image_rows, diagonal=False):
        texts = pl.ds(text_at, text_rows)
        images = pl.ds(image_at, image_rows)
        scores = scale * dot(text_low[texts, :], image_low[images, :], NT) + offset
        if diagonal:
            row = lax.broadcasted_iota(jnp.int32, scores.shape, 0)
            col = lax.broadcasted_iota(jnp.int32, scores.shape, 1)
            label = jnp.where(row == col, jnp.float32(1.0), jnp.float32(-1.0))
            values = -label * scale * (1.0 / (1.0 + jnp.exp(label * scores)))
        else:
            values = scale * (1.0 / (1.0 + jnp.exp(-scores)))
        coef[texts, images] = values.astype(jnp.bfloat16)

    def terms(texts):
        return jnp.dot(coef[texts, :], image_low[...], preferred_element_type=jnp.float32)

    fill(0, rows, 0, rows, diagonal=True)

    @pl.when(hands_over)
    def _():
        for c in range(EARLY):
            ext_text[c].wait_send()
            partner_image[c].wait_send()
        pl.semaphore_signal(
            turn, inc=1, device_id=mate_id, device_id_type=pl.DeviceIdType.MESH
        )

    @pl.when(jnp.logical_not(leads))
    def _():
        pl.semaphore_wait(turn, 1)
        for c in range(PIECES):
            ext_text[c].start()
            partner_image[c].start()

    for copy in mate_text:
        copy.wait_recv()
    fill(rows, rows, 0, rows)
    for copy in partner_image:
        copy.wait_recv()
    fill(0, 2 * rows, rows, rows)
    near_terms = terms(pl.ds(0, 2 * rows))
    mate_send[...] = near_terms[rows:].astype(jnp.bfloat16)
    mate_terms = [
        send(mate_send.at[piece], mate_recv.at[piece], 4, c, mate_id)
        for c, piece in enumerate(pieces)
    ]
    text_part[...] = near_terms[:rows]
    for copy in ext_text:
        copy.wait_recv()
    fill(2 * rows, rows, 0, 2 * rows)
    partner_coef[...] = coef[:, rows:].T

    ext_send[...] = terms(pl.ds(2 * rows, rows)).astype(jnp.bfloat16)
    ext_terms = [
        send(ext_send.at[piece], ext_recv.at[piece], 3, c, ext_id)
        for c, piece in enumerate(pieces)
    ]
    image_send[...] = jnp.dot(
        partner_coef[...], text_low[...], preferred_element_type=jnp.float32
    ).astype(jnp.bfloat16)
    image_terms = [
        send(image_send.at[piece], image_recv.at[piece], 5, c, partner)
        for c, piece in enumerate(pieces)
    ]
    image_part[...] = dot(coef[:, :rows], text_low[...], TN)

    for c, piece in enumerate(pieces):
        mate_terms[c].wait_recv()
        ext_terms[c].wait_recv()
        direction = (
            text_part[piece, :]
            + mate_recv[piece, :].astype(jnp.float32)
            + ext_recv[piece, :].astype(jnp.float32)
        )
        text_out[piece, :] = backward_norm(text_x[piece, :], text_inv[piece, :], direction)
        image_terms[c].wait_recv()
        direction = image_part[piece, :] + image_recv[piece, :].astype(jnp.float32)
        image_out[piece, :] = backward_norm(image_x[piece, :], image_inv[piece, :], direction)

    @pl.when(jnp.logical_not(hands_over))
    def _():
        for c in range(EARLY):
            ext_text[c].wait_send()
            partner_image[c].wait_send()

    for copies in (
        ext_text[EARLY:], partner_image[EARLY:], mate_text, ext_terms, mate_terms, image_terms
    ):
        for copy in copies:
            copy.wait_send()


def store(image_ref, text_ref, image_out, text_out, sem):
    step = image_ref.shape[0] // PIECES
    copies = []
    for c in range(PIECES):
        piece = pl.ds(c * step, step)
        copies += [
            pltpu.make_async_copy(image_ref.at[piece], image_out.at[piece], sem.at[0, c]),
            pltpu.make_async_copy(text_ref.at[piece], text_out.at[piece], sem.at[1, c]),
        ]
    for copy in copies:
        copy.start()
    for copy in copies:
        copy.wait()


def shards(groups, image, text, scale, offset):
    rows, width = image.shape
    full = pltpu.VMEM
    f32, low = jnp.float32, jnp.bfloat16
    image = pltpu.with_memory_space_constraint(image, pltpu.HBM)
    text = pltpu.with_memory_space_constraint(text, pltpu.HBM)
    grads = pl.pallas_call(
        functools.partial(kernel, groups, rows),
        out_shape=(jax.ShapeDtypeStruct((rows, width), f32),) * 2,
        in_specs=[pl.BlockSpec(memory_space=pltpu.SMEM)] * 2
        + [pl.BlockSpec(memory_space=pltpu.HBM)] * 2,
        out_specs=(pl.BlockSpec(memory_space=pltpu.VMEM),) * 2,
        scratch_shapes=[
            full((rows, width), f32),
            full((rows, width), f32),
            full((rows, 1), f32),
            full((rows, 1), f32),
            full((2 * rows, width), low),
            full((3 * rows, width), low),
            full((3 * rows, 2 * rows), low),
            full((rows, 3 * rows), low),
            full((rows, width), f32),
            full((rows, width), f32),
        ]
        + [full((rows, width), low)] * 6
        + [
            pltpu.SemaphoreType.DMA((2, PIECES)),
            pltpu.SemaphoreType.DMA((6, PIECES)),
            pltpu.SemaphoreType.DMA((6, PIECES)),
            pltpu.SemaphoreType.REGULAR,
        ],
        compiler_params=pltpu.CompilerParams(
            collective_id=0, has_side_effects=True, vmem_limit_bytes=32 * 1024 * 1024
        ),
        cost_estimate=pl.CostEstimate(
            flops=36 * rows * rows * width,
            bytes_accessed=16 * rows * width,
            transcendentals=6 * rows * rows,
        ),
    )(scale.reshape(1, 1), offset.reshape(1, 1), image, text)
    return tuple(
        pl.pallas_call(
            store,
            out_shape=(jax.ShapeDtypeStruct((rows, width), f32),) * 2,
            in_specs=[pl.BlockSpec(memory_space=pl.ANY)] * 2,
            out_specs=(pl.BlockSpec(memory_space=pltpu.HBM),) * 2,
            scratch_shapes=[pltpu.SemaphoreType.DMA((2, PIECES))],
            compiler_params=pltpu.CompilerParams(vmem_limit_bytes=16 * 1024 * 1024),
        )(*grads)
    )


def solution(mesh):
    if mesh.shape["sub"] != 2 or mesh.shape["dp"] % 4 or mesh.shape["dp"] < 4:
        raise ValueError("unsupported mesh")
    placed = (P(("dp", "sub"), None), P(("dp", "sub"), None), P(), P())
    return jax.shard_map(
        functools.partial(shards, mesh.shape["dp"]),
        mesh=mesh,
        in_specs=placed,
        out_specs=(P(("dp", "sub"), None), P(("dp", "sub"), None)),
        check_vma=False,
    )
```

```python
import functools

import jax
import jax.numpy as jnp
from jax import lax
from jax.experimental import pallas as pl
from jax.experimental.pallas import tpu as pltpu
from jax.sharding import PartitionSpec as P

PIECES = 4
EARLY = 2
NT = (((1,), (1,)), ((), ()))
TN = (((0,), (0,)), ((), ()))


def dot(a, b, dims):
    return lax.dot_general(a, b, dims, preferred_element_type=jnp.float32)


def inverse_norm(values):
    return lax.rsqrt(jnp.sum(values * values, axis=-1, keepdims=True) + 1e-06)


def backward_norm(values, inverse, direction):
    unit = values * inverse
    return (direction - unit * jnp.sum(unit * direction, axis=-1, keepdims=True)) * inverse


def kernel(
    groups, rows,
    scale_ref, offset_ref, image_hbm, text_hbm,
    image_out, text_out,
    image_x, text_x, image_inv, text_inv,
    image_low, text_low, coef, partner_coef,
    image_part, text_part,
    image_send, mate_send, ext_send,
    image_recv, mate_recv, ext_recv,
    load_sem, send_sem, recv_sem, turn,
):
    g = lax.axis_index("dp")
    s = lax.axis_index("sub")
    odd = lax.rem(g, 2)
    mate = g + 1 - 2 * odd
    ext = lax.rem(g - 1 + 2 * odd + groups, groups)
    partner = (g, 1 - s)
    mate_id = (mate, s)
    ext_id = (ext, s)

    near = jnp.logical_and(lax.rem((g + 1) // 2, 2) == 1, g != groups - 2)
    leads = jnp.logical_or(near, g == groups - 1)

    step = rows // PIECES
    pieces = [pl.ds(c * step, step) for c in range(PIECES)]

    barrier = pltpu.get_barrier_semaphore()
    for who in (partner, mate_id, ext_id):
        pl.semaphore_signal(barrier, inc=1, device_id=who, device_id_type=pl.DeviceIdType.MESH)

    loads = []
    for c, piece in enumerate(pieces):
        pair = (
            pltpu.make_async_copy(text_hbm.at[piece], text_x.at[piece], load_sem.at[0, c]),
            pltpu.make_async_copy(image_hbm.at[piece], image_x.at[piece], load_sem.at[1, c]),
        )
        for copy in pair:
            copy.start()
        loads.append(pair)

    def remote(src, dst, kind, c, who):
        return pltpu.make_async_remote_copy(
            src_ref=src,
            dst_ref=dst,
            send_sem=send_sem.at[kind, c],
            recv_sem=recv_sem.at[kind, c],
            device_id=who,
            device_id_type=pl.DeviceIdType.MESH,
        )

    def send(*args):
        copy = remote(*args)
        copy.start()
        return copy

    ext_text, mate_text, partner_image = [], [], []
    for c, piece in enumerate(pieces):
        loads[c][0].wait()
        values = text_x[piece, :]
        inverse = inverse_norm(values)
        text_inv[piece, :] = inverse
        text_low[piece, :] = (values * inverse).astype(jnp.bfloat16)
        if c == 0:
            pl.semaphore_wait(barrier, 3)
        own = text_low.at[piece]
        ext_text.append(remote(own, text_low.at[pl.ds(2 * rows + c * step, step)], 0, c, ext_id))
        pl.when(leads)(ext_text[c].start)
        mate_text.append(send(own, text_low.at[pl.ds(rows + c * step, step)], 1, c, mate_id))
        loads[c][1].wait()
        values = image_x[piece, :]
        inverse = inverse_norm(values)
        image_inv[piece, :] = inverse
        image_low[piece, :] = (values * inverse).astype(jnp.bfloat16)
        own = image_low.at[piece]
        partner_image.append(remote(own, image_low.at[pl.ds(rows + c * step, step)], 2, c, partner))
        pl.when(leads)(partner_image[c].start)

    scale = scale_ref[0, 0]
    offset = offset_ref[0, 0]

    def fill(text_at, text_rows, image_at, image_rows, diagonal=False):
        texts = pl.ds(text_at, text_rows)
        images = pl.ds(image_at, image_rows)
        scores = scale * dot(text_low[texts, :], image_low[images, :], NT) + offset
        if diagonal:
            row = lax.broadcasted_iota(jnp.int32, scores.shape, 0)
            col = lax.broadcasted_iota(jnp.int32, scores.shape, 1)
            label = jnp.where(row == col, jnp.float32(1.0), jnp.float32(-1.0))
            values = -label * scale * (1.0 / (1.0 + jnp.exp(label * scores)))
        else:
            values = scale * (1.0 / (1.0 + jnp.exp(-scores)))
        coef[texts, images] = values.astype(jnp.bfloat16)

    def terms(texts):
        return jnp.dot(coef[texts, :], image_low[...], preferred_element_type=jnp.float32)

    fill(0, rows, 0, rows, diagonal=True)

    @pl.when(leads)
    def _():
        for c in range(EARLY):
            ext_text[c].wait_send()
            partner_image[c].wait_send()
        pl.semaphore_signal(
            turn, inc=1, device_id=mate_id, device_id_type=pl.DeviceIdType.MESH
        )

    @pl.when(jnp.logical_not(leads))
    def _():
        pl.semaphore_wait(turn, 1)
        for c in range(PIECES):
            ext_text[c].start()
            partner_image[c].start()

    for copy in mate_text:
        copy.wait_recv()
    fill(rows, rows, 0, rows)
    for copy in partner_image:
        copy.wait_recv()
    fill(0, 2 * rows, rows, rows)
    for copy in ext_text:
        copy.wait_recv()
    fill(2 * rows, rows, 0, 2 * rows)
    partner_coef[...] = coef[:, rows:].T

    ext_send[...] = terms(pl.ds(2 * rows, rows)).astype(jnp.bfloat16)
    ext_terms = [
        send(ext_send.at[piece], ext_recv.at[piece], 3, c, ext_id)
        for c, piece in enumerate(pieces)
    ]
    image_send[...] = jnp.dot(
        partner_coef[...], text_low[...], preferred_element_type=jnp.float32
    ).astype(jnp.bfloat16)
    image_terms = [
        send(image_send.at[piece], image_recv.at[piece], 5, c, partner)
        for c, piece in enumerate(pieces)
    ]
    near_terms = terms(pl.ds(0, 2 * rows))
    mate_send[...] = near_terms[rows:].astype(jnp.bfloat16)
    mate_terms = [
        send(mate_send.at[piece], mate_recv.at[piece], 4, c, mate_id)
        for c, piece in enumerate(pieces)
    ]
    text_part[...] = near_terms[:rows]
    image_part[...] = dot(coef[:, :rows], text_low[...], TN)

    for c, piece in enumerate(pieces):
        mate_terms[c].wait_recv()
        ext_terms[c].wait_recv()
        direction = (
            text_part[piece, :]
            + mate_recv[piece, :].astype(jnp.float32)
            + ext_recv[piece, :].astype(jnp.float32)
        )
        text_out[piece, :] = backward_norm(text_x[piece, :], text_inv[piece, :], direction)
        image_terms[c].wait_recv()
        direction = image_part[piece, :] + image_recv[piece, :].astype(jnp.float32)
        image_out[piece, :] = backward_norm(image_x[piece, :], image_inv[piece, :], direction)

    @pl.when(jnp.logical_not(leads))
    def _():
        for c in range(EARLY):
            ext_text[c].wait_send()
            partner_image[c].wait_send()

    for copies in (
        ext_text[EARLY:], partner_image[EARLY:], mate_text, ext_terms, mate_terms, image_terms
    ):
        for copy in copies:
            copy.wait_send()


def store(image_ref, text_ref, image_out, text_out, sem):
    step = image_ref.shape[0] // PIECES
    copies = []
    for c in range(PIECES):
        piece = pl.ds(c * step, step)
        copies += [
            pltpu.make_async_copy(image_ref.at[piece], image_out.at[piece], sem.at[0, c]),
            pltpu.make_async_copy(text_ref.at[piece], text_out.at[piece], sem.at[1, c]),
        ]
    for copy in copies:
        copy.start()
    for copy in copies:
        copy.wait()


def shards(groups, image, text, scale, offset):
    rows, width = image.shape
    full = pltpu.VMEM
    f32, low = jnp.float32, jnp.bfloat16
    image = pltpu.with_memory_space_constraint(image, pltpu.HBM)
    text = pltpu.with_memory_space_constraint(text, pltpu.HBM)
    grads = pl.pallas_call(
        functools.partial(kernel, groups, rows),
        out_shape=(jax.ShapeDtypeStruct((rows, width), f32),) * 2,
        in_specs=[pl.BlockSpec(memory_space=pltpu.SMEM)] * 2
        + [pl.BlockSpec(memory_space=pltpu.HBM)] * 2,
        out_specs=(pl.BlockSpec(memory_space=pltpu.VMEM),) * 2,
        scratch_shapes=[
            full((rows, width), f32),
            full((rows, width), f32),
            full((rows, 1), f32),
            full((rows, 1), f32),
            full((2 * rows, width), low),
            full((3 * rows, width), low),
            full((3 * rows, 2 * rows), low),
            full((rows, 3 * rows), low),
            full((rows, width), f32),
            full((rows, width), f32),
        ]
        + [full((rows, width), low)] * 6
        + [
            pltpu.SemaphoreType.DMA((2, PIECES)),
            pltpu.SemaphoreType.DMA((6, PIECES)),
            pltpu.SemaphoreType.DMA((6, PIECES)),
            pltpu.SemaphoreType.REGULAR,
        ],
        compiler_params=pltpu.CompilerParams(
            collective_id=0, has_side_effects=True, vmem_limit_bytes=32 * 1024 * 1024
        ),
        cost_estimate=pl.CostEstimate(
            flops=36 * rows * rows * width,
            bytes_accessed=16 * rows * width,
            transcendentals=6 * rows * rows,
        ),
    )(scale.reshape(1, 1), offset.reshape(1, 1), image, text)
    return tuple(
        pl.pallas_call(
            store,
            out_shape=(jax.ShapeDtypeStruct((rows, width), f32),) * 2,
            in_specs=[pl.BlockSpec(memory_space=pl.ANY)] * 2,
            out_specs=(pl.BlockSpec(memory_space=pltpu.HBM),) * 2,
            scratch_shapes=[pltpu.SemaphoreType.DMA((2, PIECES))],
            compiler_params=pltpu.CompilerParams(vmem_limit_bytes=16 * 1024 * 1024),
        )(*grads)
    )


def solution(mesh):
    if mesh.shape["sub"] != 2 or mesh.shape["dp"] % 4 or mesh.shape["dp"] < 4:
        raise ValueError("unsupported mesh")
    placed = (P(("dp", "sub"), None), P(("dp", "sub"), None), P(), P())
    return jax.shard_map(
        functools.partial(shards, mesh.shape["dp"]),
        mesh=mesh,
        in_specs=placed,
        out_specs=(P(("dp", "sub"), None), P(("dp", "sub"), None)),
        check_vma=False,
    )
```

```python
import functools

import jax
import jax.numpy as jnp
from jax import lax
from jax.experimental import pallas as pl
from jax.experimental.pallas import tpu as pltpu
from jax.sharding import PartitionSpec as P

PIECES = 4
EARLY = 3
NT = (((1,), (1,)), ((), ()))
TN = (((0,), (0,)), ((), ()))


def dot(a, b, dims):
    return lax.dot_general(a, b, dims, preferred_element_type=jnp.float32)


def inverse_norm(values):
    return lax.rsqrt(jnp.sum(values * values, axis=-1, keepdims=True) + 1e-06)


def backward_norm(values, inverse, direction):
    unit = values * inverse
    return (direction - unit * jnp.sum(unit * direction, axis=-1, keepdims=True)) * inverse


def kernel(
    groups, rows,
    scale_ref, offset_ref, image_hbm, text_hbm,
    image_out, text_out,
    image_x, text_x, image_inv, text_inv,
    image_low, text_low, coef, partner_coef,
    image_part, text_part,
    image_send, mate_send, ext_send,
    image_recv, mate_recv, ext_recv,
    load_sem, send_sem, recv_sem, turn,
):
    g = lax.axis_index("dp")
    s = lax.axis_index("sub")
    odd = lax.rem(g, 2)
    mate = g + 1 - 2 * odd
    ext = lax.rem(g - 1 + 2 * odd + groups, groups)
    partner = (g, 1 - s)
    mate_id = (mate, s)
    ext_id = (ext, s)

    leads = jnp.logical_or(lax.rem((g + 1) // 2, 2) == 1, g == groups - 1)
    hands_over = jnp.logical_and(leads, g < groups - 2)

    step = rows // PIECES
    pieces = [pl.ds(c * step, step) for c in range(PIECES)]

    barrier = pltpu.get_barrier_semaphore()
    for who in (partner, mate_id, ext_id):
        pl.semaphore_signal(barrier, inc=1, device_id=who, device_id_type=pl.DeviceIdType.MESH)

    loads = []
    for c, piece in enumerate(pieces):
        pair = (
            pltpu.make_async_copy(text_hbm.at[piece], text_x.at[piece], load_sem.at[0, c]),
            pltpu.make_async_copy(image_hbm.at[piece], image_x.at[piece], load_sem.at[1, c]),
        )
        for copy in pair:
            copy.start()
        loads.append(pair)

    def remote(src, dst, kind, c, who):
        return pltpu.make_async_remote_copy(
            src_ref=src,
            dst_ref=dst,
            send_sem=send_sem.at[kind, c],
            recv_sem=recv_sem.at[kind, c],
            device_id=who,
            device_id_type=pl.DeviceIdType.MESH,
        )

    def send(*args):
        copy = remote(*args)
        copy.start()
        return copy

    ext_text, mate_text, partner_image = [], [], []
    for c, piece in enumerate(pieces):
        loads[c][0].wait()
        values = text_x[piece, :]
        inverse = inverse_norm(values)
        text_inv[piece, :] = inverse
        text_low[piece, :] = (values * inverse).astype(jnp.bfloat16)
        if c == 0:
            pl.semaphore_wait(barrier, 3)
        own = text_low.at[piece]
        ext_text.append(remote(own, text_low.at[pl.ds(2 * rows + c * step, step)], 0, c, ext_id))
        pl.when(leads)(ext_text[c].start)
        mate_text.append(send(own, text_low.at[pl.ds(rows + c * step, step)], 1, c, mate_id))
        loads[c][1].wait()
        values = image_x[piece, :]
        inverse = inverse_norm(values)
        image_inv[piece, :] = inverse
        image_low[piece, :] = (values * inverse).astype(jnp.bfloat16)
        own = image_low.at[piece]
        partner_image.append(remote(own, image_low.at[pl.ds(rows + c * step, step)], 2, c, partner))
        pl.when(leads)(partner_image[c].start)

    scale = scale_ref[0, 0]
    offset = offset_ref[0, 0]

    def fill(text_at, text_rows, image_at, image_rows, diagonal=False):
        texts = pl.ds(text_at, text_rows)
        images = pl.ds(image_at, image_rows)
        scores = scale * dot(text_low[texts, :], image_low[images, :], NT) + offset
        if diagonal:
            row = lax.broadcasted_iota(jnp.int32, scores.shape, 0)
            col = lax.broadcasted_iota(jnp.int32, scores.shape, 1)
            label = jnp.where(row == col, jnp.float32(1.0), jnp.float32(-1.0))
            values = -label * scale * (1.0 / (1.0 + jnp.exp(label * scores)))
        else:
            values = scale * (1.0 / (1.0 + jnp.exp(-scores)))
        coef[texts, images] = values.astype(jnp.bfloat16)

    def terms(texts):
        return jnp.dot(coef[texts, :], image_low[...], preferred_element_type=jnp.float32)

    fill(0, rows, 0, rows, diagonal=True)

    @pl.when(hands_over)
    def _():
        for c in range(EARLY):
            ext_text[c].wait_send()
            partner_image[c].wait_send()
        pl.semaphore_signal(
            turn, inc=1, device_id=mate_id, device_id_type=pl.DeviceIdType.MESH
        )

    @pl.when(jnp.logical_not(leads))
    def _():
        pl.semaphore_wait(turn, 1)
        for c in range(PIECES):
            ext_text[c].start()
            partner_image[c].start()

    for copy in mate_text:
        copy.wait_recv()
    fill(rows, rows, 0, rows)
    for copy in partner_image:
        copy.wait_recv()
    fill(0, 2 * rows, rows, rows)
    for copy in ext_text:
        copy.wait_recv()
    fill(2 * rows, rows, 0, 2 * rows)
    partner_coef[...] = coef[:, rows:].T

    ext_send[...] = terms(pl.ds(2 * rows, rows)).astype(jnp.bfloat16)
    ext_terms = [
        send(ext_send.at[piece], ext_recv.at[piece], 3, c, ext_id)
        for c, piece in enumerate(pieces)
    ]
    image_send[...] = jnp.dot(
        partner_coef[...], text_low[...], preferred_element_type=jnp.float32
    ).astype(jnp.bfloat16)
    image_terms = [
        send(image_send.at[piece], image_recv.at[piece], 5, c, partner)
        for c, piece in enumerate(pieces)
    ]
    near_terms = terms(pl.ds(0, 2 * rows))
    mate_send[...] = near_terms[rows:].astype(jnp.bfloat16)
    mate_terms = [
        send(mate_send.at[piece], mate_recv.at[piece], 4, c, mate_id)
        for c, piece in enumerate(pieces)
    ]
    text_part[...] = near_terms[:rows]
    image_part[...] = dot(coef[:, :rows], text_low[...], TN)

    for c, piece in enumerate(pieces):
        mate_terms[c].wait_recv()
        ext_terms[c].wait_recv()
        direction = (
            text_part[piece, :]
            + mate_recv[piece, :].astype(jnp.float32)
            + ext_recv[piece, :].astype(jnp.float32)
        )
        text_out[piece, :] = backward_norm(text_x[piece, :], text_inv[piece, :], direction)
        image_terms[c].wait_recv()
        direction = image_part[piece, :] + image_recv[piece, :].astype(jnp.float32)
        image_out[piece, :] = backward_norm(image_x[piece, :], image_inv[piece, :], direction)

    @pl.when(jnp.logical_not(hands_over))
    def _():
        for c in range(EARLY):
            ext_text[c].wait_send()
            partner_image[c].wait_send()

    for copies in (
        ext_text[EARLY:], partner_image[EARLY:], mate_text, ext_terms, mate_terms, image_terms
    ):
        for copy in copies:
            copy.wait_send()


def store(image_ref, text_ref, image_out, text_out, sem):
    step = image_ref.shape[0] // PIECES
    copies = []
    for c in range(PIECES):
        piece = pl.ds(c * step, step)
        copies += [
            pltpu.make_async_copy(image_ref.at[piece], image_out.at[piece], sem.at[0, c]),
            pltpu.make_async_copy(text_ref.at[piece], text_out.at[piece], sem.at[1, c]),
        ]
    for copy in copies:
        copy.start()
    for copy in copies:
        copy.wait()


def shards(groups, image, text, scale, offset):
    rows, width = image.shape
    full = pltpu.VMEM
    f32, low = jnp.float32, jnp.bfloat16
    image = pltpu.with_memory_space_constraint(image, pltpu.HBM)
    text = pltpu.with_memory_space_constraint(text, pltpu.HBM)
    grads = pl.pallas_call(
        functools.partial(kernel, groups, rows),
        out_shape=(jax.ShapeDtypeStruct((rows, width), f32),) * 2,
        in_specs=[pl.BlockSpec(memory_space=pltpu.SMEM)] * 2
        + [pl.BlockSpec(memory_space=pltpu.HBM)] * 2,
        out_specs=(pl.BlockSpec(memory_space=pltpu.VMEM),) * 2,
        scratch_shapes=[
            full((rows, width), f32),
            full((rows, width), f32),
            full((rows, 1), f32),
            full((rows, 1), f32),
            full((2 * rows, width), low),
            full((3 * rows, width), low),
            full((3 * rows, 2 * rows), low),
            full((rows, 3 * rows), low),
            full((rows, width), f32),
            full((rows, width), f32),
        ]
        + [full((rows, width), low)] * 6
        + [
            pltpu.SemaphoreType.DMA((2, PIECES)),
            pltpu.SemaphoreType.DMA((6, PIECES)),
            pltpu.SemaphoreType.DMA((6, PIECES)),
            pltpu.SemaphoreType.REGULAR,
        ],
        compiler_params=pltpu.CompilerParams(
            collective_id=0, has_side_effects=True, vmem_limit_bytes=32 * 1024 * 1024
        ),
        cost_estimate=pl.CostEstimate(
            flops=36 * rows * rows * width,
            bytes_accessed=16 * rows * width,
            transcendentals=6 * rows * rows,
        ),
    )(scale.reshape(1, 1), offset.reshape(1, 1), image, text)
    return tuple(
        pl.pallas_call(
            store,
            out_shape=(jax.ShapeDtypeStruct((rows, width), f32),) * 2,
            in_specs=[pl.BlockSpec(memory_space=pl.ANY)] * 2,
            out_specs=(pl.BlockSpec(memory_space=pltpu.HBM),) * 2,
            scratch_shapes=[pltpu.SemaphoreType.DMA((2, PIECES))],
            compiler_params=pltpu.CompilerParams(vmem_limit_bytes=16 * 1024 * 1024),
        )(*grads)
    )


def solution(mesh):
    if mesh.shape["sub"] != 2 or mesh.shape["dp"] % 4 or mesh.shape["dp"] < 4:
        raise ValueError("unsupported mesh")
    placed = (P(("dp", "sub"), None), P(("dp", "sub"), None), P(), P())
    return jax.shard_map(
        functools.partial(shards, mesh.shape["dp"]),
        mesh=mesh,
        in_specs=placed,
        out_specs=(P(("dp", "sub"), None), P(("dp", "sub"), None)),
        check_vma=False,
    )
```

```python
import functools

import jax
import jax.numpy as jnp
from jax import lax
from jax.experimental import pallas as pl
from jax.experimental.pallas import tpu as pltpu
from jax.sharding import PartitionSpec as P

PIECES = 4
EARLY = 2
NT = (((1,), (1,)), ((), ()))
TN = (((0,), (0,)), ((), ()))


def dot(a, b, dims):
    return lax.dot_general(a, b, dims, preferred_element_type=jnp.float32)


def inverse_norm(values):
    return lax.rsqrt(jnp.sum(values * values, axis=-1, keepdims=True) + 1e-06)


def backward_norm(values, inverse, direction):
    unit = values * inverse
    return (direction - unit * jnp.sum(unit * direction, axis=-1, keepdims=True)) * inverse


def kernel(
    groups, rows,
    scale_ref, offset_ref, image_hbm, text_hbm,
    image_out, text_out,
    image_x, text_x, image_inv, text_inv,
    image_low, text_low, coef, partner_coef,
    image_part, text_part,
    image_send, mate_send, ext_send,
    image_recv, mate_recv, ext_recv,
    load_sem, send_sem, recv_sem, turn,
):
    g = lax.axis_index("dp")
    s = lax.axis_index("sub")
    odd = lax.rem(g, 2)
    mate = g + 1 - 2 * odd
    ext = lax.rem(g - 1 + 2 * odd + groups, groups)
    partner = (g, 1 - s)
    mate_id = (mate, s)
    ext_id = (ext, s)

    wrap = jnp.logical_or(g == 0, g == groups - 1)
    near = jnp.logical_and(lax.rem((g + 1) // 2, 2) == 1, g != groups - 2)
    leads = jnp.logical_or(near, wrap)
    hands_over = jnp.logical_and(leads, g > 1)

    step = rows // PIECES
    pieces = [pl.ds(c * step, step) for c in range(PIECES)]

    barrier = pltpu.get_barrier_semaphore()
    for who in (partner, mate_id, ext_id):
        pl.semaphore_signal(barrier, inc=1, device_id=who, device_id_type=pl.DeviceIdType.MESH)

    loads = []
    for c, piece in enumerate(pieces):
        pair = (
            pltpu.make_async_copy(text_hbm.at[piece], text_x.at[piece], load_sem.at[0, c]),
            pltpu.make_async_copy(image_hbm.at[piece], image_x.at[piece], load_sem.at[1, c]),
        )
        for copy in pair:
            copy.start()
        loads.append(pair)

    def remote(src, dst, kind, c, who):
        return pltpu.make_async_remote_copy(
            src_ref=src,
            dst_ref=dst,
            send_sem=send_sem.at[kind, c],
            recv_sem=recv_sem.at[kind, c],
            device_id=who,
            device_id_type=pl.DeviceIdType.MESH,
        )

    def send(*args):
        copy = remote(*args)
        copy.start()
        return copy

    ext_text, mate_text, partner_image = [], [], []
    for c, piece in enumerate(pieces):
        loads[c][0].wait()
        values = text_x[piece, :]
        inverse = inverse_norm(values)
        text_inv[piece, :] = inverse
        text_low[piece, :] = (values * inverse).astype(jnp.bfloat16)
        if c == 0:
            pl.semaphore_wait(barrier, 3)
        own = text_low.at[piece]
        ext_text.append(remote(own, text_low.at[pl.ds(2 * rows + c * step, step)], 0, c, ext_id))
        pl.when(leads)(ext_text[c].start)
        mate_text.append(send(own, text_low.at[pl.ds(rows + c * step, step)], 1, c, mate_id))
        loads[c][1].wait()
        values = image_x[piece, :]
        inverse = inverse_norm(values)
        image_inv[piece, :] = inverse
        image_low[piece, :] = (values * inverse).astype(jnp.bfloat16)
        own = image_low.at[piece]
        partner_image.append(remote(own, image_low.at[pl.ds(rows + c * step, step)], 2, c, partner))
        pl.when(leads)(partner_image[c].start)

    scale = scale_ref[0, 0]
    offset = offset_ref[0, 0]

    def fill(text_at, text_rows, image_at, image_rows, diagonal=False):
        texts = pl.ds(text_at, text_rows)
        images = pl.ds(image_at, image_rows)
        scores = scale * dot(text_low[texts, :], image_low[images, :], NT) + offset
        if diagonal:
            row = lax.broadcasted_iota(jnp.int32, scores.shape, 0)
            col = lax.broadcasted_iota(jnp.int32, scores.shape, 1)
            label = jnp.where(row == col, jnp.float32(1.0), jnp.float32(-1.0))
            values = -label * scale * (1.0 / (1.0 + jnp.exp(label * scores)))
        else:
            values = scale * (1.0 / (1.0 + jnp.exp(-scores)))
        coef[texts, images] = values.astype(jnp.bfloat16)

    def terms(texts):
        return jnp.dot(coef[texts, :], image_low[...], preferred_element_type=jnp.float32)

    fill(0, rows, 0, rows, diagonal=True)

    @pl.when(hands_over)
    def _():
        for c in range(EARLY):
            ext_text[c].wait_send()
            partner_image[c].wait_send()
        pl.semaphore_signal(
            turn, inc=1, device_id=mate_id, device_id_type=pl.DeviceIdType.MESH
        )

    @pl.when(jnp.logical_not(leads))
    def _():
        pl.semaphore_wait(turn, 1)
        for c in range(PIECES):
            ext_text[c].start()
            partner_image[c].start()

    for copy in mate_text:
        copy.wait_recv()
    fill(rows, rows, 0, rows)
    for copy in partner_image:
        copy.wait_recv()
    fill(0, 2 * rows, rows, rows)
    for copy in ext_text:
        copy.wait_recv()
    fill(2 * rows, rows, 0, 2 * rows)
    partner_coef[...] = coef[:, rows:].T

    ext_send[...] = terms(pl.ds(2 * rows, rows)).astype(jnp.bfloat16)
    ext_terms = [
        send(ext_send.at[piece], ext_recv.at[piece], 3, c, ext_id)
        for c, piece in enumerate(pieces)
    ]
    image_send[...] = jnp.dot(
        partner_coef[...], text_low[...], preferred_element_type=jnp.float32
    ).astype(jnp.bfloat16)
    image_terms = [
        send(image_send.at[piece], image_recv.at[piece], 5, c, partner)
        for c, piece in enumerate(pieces)
    ]
    near_terms = terms(pl.ds(0, 2 * rows))
    mate_send[...] = near_terms[rows:].astype(jnp.bfloat16)
    mate_terms = [
        send(mate_send.at[piece], mate_recv.at[piece], 4, c, mate_id)
        for c, piece in enumerate(pieces)
    ]
    text_part[...] = near_terms[:rows]
    image_part[...] = dot(coef[:, :rows], text_low[...], TN)

    for c, piece in enumerate(pieces):
        image_terms[c].wait_recv()
        direction = image_part[piece, :] + image_recv[piece, :].astype(jnp.float32)
        image_out[piece, :] = backward_norm(image_x[piece, :], image_inv[piece, :], direction)
    for c, piece in enumerate(pieces):
        mate_terms[c].wait_recv()
        ext_terms[c].wait_recv()
        direction = (
            text_part[piece, :]
            + mate_recv[piece, :].astype(jnp.float32)
            + ext_recv[piece, :].astype(jnp.float32)
        )
        text_out[piece, :] = backward_norm(text_x[piece, :], text_inv[piece, :], direction)

    @pl.when(jnp.logical_not(hands_over))
    def _():
        for c in range(EARLY):
            ext_text[c].wait_send()
            partner_image[c].wait_send()

    for copies in (
        ext_text[EARLY:], partner_image[EARLY:], mate_text, ext_terms, mate_terms, image_terms
    ):
        for copy in copies:
            copy.wait_send()


def store(image_ref, text_ref, image_out, text_out, sem):
    step = image_ref.shape[0] // PIECES
    copies = []
    for c in range(PIECES):
        piece = pl.ds(c * step, step)
        copies += [
            pltpu.make_async_copy(image_ref.at[piece], image_out.at[piece], sem.at[0, c]),
            pltpu.make_async_copy(text_ref.at[piece], text_out.at[piece], sem.at[1, c]),
        ]
    for copy in copies:
        copy.start()
    for copy in copies:
        copy.wait()


def shards(groups, image, text, scale, offset):
    rows, width = image.shape
    full = pltpu.VMEM
    f32, low = jnp.float32, jnp.bfloat16
    image = pltpu.with_memory_space_constraint(image, pltpu.HBM)
    text = pltpu.with_memory_space_constraint(text, pltpu.HBM)
    grads = pl.pallas_call(
        functools.partial(kernel, groups, rows),
        out_shape=(jax.ShapeDtypeStruct((rows, width), f32),) * 2,
        in_specs=[pl.BlockSpec(memory_space=pltpu.SMEM)] * 2
        + [pl.BlockSpec(memory_space=pltpu.HBM)] * 2,
        out_specs=(pl.BlockSpec(memory_space=pltpu.VMEM),) * 2,
        scratch_shapes=[
            full((rows, width), f32),
            full((rows, width), f32),
            full((rows, 1), f32),
            full((rows, 1), f32),
            full((2 * rows, width), low),
            full((3 * rows, width), low),
            full((3 * rows, 2 * rows), low),
            full((rows, 3 * rows), low),
            full((rows, width), f32),
            full((rows, width), f32),
        ]
        + [full((rows, width), low)] * 6
        + [
            pltpu.SemaphoreType.DMA((2, PIECES)),
            pltpu.SemaphoreType.DMA((6, PIECES)),
            pltpu.SemaphoreType.DMA((6, PIECES)),
            pltpu.SemaphoreType.REGULAR,
        ],
        compiler_params=pltpu.CompilerParams(
            collective_id=0, has_side_effects=True, vmem_limit_bytes=32 * 1024 * 1024
        ),
        cost_estimate=pl.CostEstimate(
            flops=36 * rows * rows * width,
            bytes_accessed=16 * rows * width,
            transcendentals=6 * rows * rows,
        ),
    )(scale.reshape(1, 1), offset.reshape(1, 1), image, text)
    return tuple(
        pl.pallas_call(
            store,
            out_shape=(jax.ShapeDtypeStruct((rows, width), f32),) * 2,
            in_specs=[pl.BlockSpec(memory_space=pl.ANY)] * 2,
            out_specs=(pl.BlockSpec(memory_space=pltpu.HBM),) * 2,
            scratch_shapes=[pltpu.SemaphoreType.DMA((2, PIECES))],
            compiler_params=pltpu.CompilerParams(vmem_limit_bytes=16 * 1024 * 1024),
        )(*grads)
    )


def solution(mesh):
    if mesh.shape["sub"] != 2 or mesh.shape["dp"] % 4 or mesh.shape["dp"] < 4:
        raise ValueError("unsupported mesh")
    placed = (P(("dp", "sub"), None), P(("dp", "sub"), None), P(), P())
    return jax.shard_map(
        functools.partial(shards, mesh.shape["dp"]),
        mesh=mesh,
        in_specs=placed,
        out_specs=(P(("dp", "sub"), None), P(("dp", "sub"), None)),
        check_vma=False,
    )
```
